128 devices in a mesh: frame: 8 (over z_hi, x), patch: 16 (over y, z_lo, core).
Axes of the slice: x: 4, y: 4, z: 4 (z_hi: 2, z_lo: 2; z = z_hi * 2 + z_lo), core: 2. Of those that a mesh axis runs over, the one named last changes fastest.
Arguments:
- tokens: bfloat16 [32, 1536, 1152], P('frame', 'patch'), may hold values from -6 to 6
- modulation: float32 [2, 3, 1152], replicated, may hold values from -0.5 to 1
- spatial_input: bfloat16 [1152, 3456], replicated, may hold values from -4 to 4
- spatial_output: bfloat16 [1152, 1152], replicated, may hold values from -0.1875 to 0.1875
- temporal_input: bfloat16 [1152, 3456], replicated, may hold values from -4 to 4
- temporal_output: bfloat16 [1152, 1152], replicated, may hold values from -0.1875 to 0.1875
Outputs:
- result: bfloat16 [32, 1536, 1152], P('frame', 'patch')
The draws below stay inside these ranges and needn't reach their ends.
All inputs are finite; a program needn't handle non-finite values.
Results may differ from the reference program's by a relative error of at most 0.03.
The reference program's roundings to bfloat16 on the way count: a program that leaves them out, or rounds other values in their place, can miss the bound.
Values may be sent and summed in bfloat16 or wider, within the bound.
A program may use at most 320 MiB of HBM per device.

```python
import math
import jax
import jax.numpy as jnp
from jax import lax

D = 1152
HEADS = 16
HEAD = 72
FRAMES = 32
PATCHES = 1536


def drawn_matrix(key):
    base = jax.random.normal(key, (D, 3 * D), jnp.float32) / math.sqrt(D)
    factor = jnp.where(jnp.arange(3 * D) < 2 * D, 2.0, 1.0)[None, :]
    return jnp.clip(base * factor, -4.0, 4.0).astype(jnp.bfloat16)


def draw_tokens(key, part):
    key = jax.random.fold_in(key, 1)
    base_key = jax.random.fold_in(key, 0)
    shape = (FRAMES, PATCHES, D)
    whole = jnp.clip(0.5 * jax.random.normal(base_key, shape, jnp.float32), -6.0, 6.0)
    return whole.astype(jnp.bfloat16)


def draw_spatial_input(key, part):
    key = jax.random.fold_in(key, 2)
    return drawn_matrix(key)


def draw_temporal_input(key, part):
    key = jax.random.fold_in(key, 3)
    return drawn_matrix(key)


def centred(stream_key, dims, width, most, kind=jnp.bfloat16):
    array = width * jax.random.normal(stream_key, dims, jnp.float32)
    return jnp.clip(array, min=-most, max=most).astype(kind)


def setup_inputs(seed: int = 0) -> dict:
    arg_keys = jax.random.split(jax.random.key(seed), 7)
    tokens = draw_tokens(jax.random.fold_in(arg_keys[6], 71), 0)
    modulation = jnp.clip(jax.random.uniform(arg_keys[1], (2, 3, D), jnp.float32, -0.5, 1.0), -0.5, 1.0)
    spatial_input = draw_spatial_input(jax.random.fold_in(arg_keys[6], 71), 0)
    spatial_output = centred(arg_keys[3], (D, D), D ** -0.5, 0.1875)
    temporal_input = draw_temporal_input(jax.random.fold_in(arg_keys[6], 71), 0)
    temporal_output = centred(arg_keys[5], (D, D), D ** -0.5, 0.1875)
    return dict(tokens=tokens, modulation=modulation, spatial_input=spatial_input, spatial_output=spatial_output, temporal_input=temporal_input, temporal_output=temporal_output)


def modulate(values, table):
    wide = values.astype(jnp.float32)
    centre = lax.optimization_barrier(jnp.mean(wide, axis=-1, keepdims=True))
    spread = lax.optimization_barrier(jnp.mean(jnp.square(wide - centre), axis=-1, keepdims=True))
    normed = (wide - centre) * lax.rsqrt(spread + 1e-06)
    return (normed * (1.0 + table[1]) + table[0]).astype(jnp.bfloat16)

def project_in(mixed, weights):
    lead = mixed.shape[:-1]
    flat = jnp.dot(mixed.reshape(-1, D), weights, preferred_element_type=jnp.float32)
    return flat.astype(jnp.bfloat16).reshape(lead + (3, HEADS, HEAD))

def softmax_rows(scores):
    top = lax.optimization_barrier(jnp.max(scores, axis=-1, keepdims=True))
    expo = jnp.exp(scores - top)
    return (expo / lax.optimization_barrier(jnp.sum(expo, axis=-1, keepdims=True))).astype(jnp.bfloat16)

def residual(values, attended, weights, table):
    flat = jnp.dot(attended.reshape(-1, D), weights, preferred_element_type=jnp.float32)
    return (values.astype(jnp.float32) + table[2] * flat.reshape(values.shape)).astype(jnp.bfloat16)

def spatial_frame(packed):
    queries = packed[:, 0].astype(jnp.float32)
    keys = packed[:, 1].astype(jnp.float32)
    values = packed[:, 2].astype(jnp.float32)
    scores = jnp.einsum('qhe,khe->hqk', queries, keys) / math.sqrt(HEAD)
    weights = softmax_rows(scores)
    return jnp.einsum('hqk,khe->qhe', weights.astype(jnp.float32), values).astype(jnp.bfloat16)

def reference(tokens, modulation, spatial_input, spatial_output, temporal_input, temporal_output):
    packed = project_in(modulate(tokens, modulation[0]), spatial_input)
    attended = lax.map(spatial_frame, packed)
    updated = residual(tokens, attended, spatial_output, modulation[0])
    packed = project_in(modulate(updated, modulation[1]), temporal_input)
    queries = packed[:, :, 0].astype(jnp.float32)
    keys = packed[:, :, 1].astype(jnp.float32)
    values = packed[:, :, 2].astype(jnp.float32)
    scores = jnp.einsum('qphe,kphe->phqk', queries, keys) / math.sqrt(HEAD)
    weights = softmax_rows(scores)
    attended = jnp.einsum('phqk,kphe->qphe', weights.astype(jnp.float32), values).astype(jnp.bfloat16)
    return residual(updated, attended, temporal_output, modulation[1])
```

```python
import functools
import math

import jax
import jax.numpy as jnp
from jax import lax
from jax.experimental import pallas as pl
from jax.experimental.pallas import tpu as pltpu
from jax.sharding import PartitionSpec as P

D = 1152
HEADS = 16
HEAD = 72
WIN = 640
SCALE = math.log2(math.e) / math.sqrt(HEAD)
MESH = pl.DeviceIdType.MESH
VMEM_LIMIT = 60 * 1024 * 1024
ORDER = (0, 1, 3, 2)


def modulate(values, table):
    wide = values.astype(jnp.float32)
    centre = jnp.mean(wide, axis=-1, keepdims=True)
    wide = wide - centre
    spread = jnp.mean(jnp.square(wide), axis=-1, keepdims=True)
    normed = wide * lax.rsqrt(spread + 1e-06)
    return (normed * (1.0 + table[1:2]) + table[0:1]).astype(jnp.bfloat16)


def nt_dot(a, b):
    return lax.dot_general(a, b, (((1,), (1,)), ((), ())), preferred_element_type=jnp.float32)


def nn_dot(a, b):
    return jnp.dot(a, b, preferred_element_type=jnp.float32)


def head_attention(queries, keys, values, start, free, bias=None):
    lane = lax.broadcasted_iota(jnp.int32, (1, 256), 1)
    mine = (lane >= start) & (lane < start + HEAD)
    one = jnp.where(lane == free, 1.0, 0.0)
    chosen = queries * jnp.where(mine, 1.0, 0.0).astype(jnp.bfloat16)
    counted = values * (1.0 - one).astype(jnp.bfloat16) + one.astype(jnp.bfloat16)
    scores = nt_dot(chosen, keys)
    if bias is not None:
        scores = scores + bias
    top = jnp.max(scores, axis=-1, keepdims=True)
    weights = jnp.exp2(scores - top).astype(jnp.bfloat16)
    mixed = nn_dot(weights, counted)
    mixed = mixed * (1.0 / mixed[:, free : free + 1])
    return jnp.where(mine, mixed, 0.0)


def spatial_kernel(
    tok, mod, w_in, w_out, out,
    x, w, wo, q, k, v, att, att_in, u,
    load_sem, y_send, y_recv, s_send, s_recv, z_send, z_recv, a_send, a_recv, r_send, r_recv, o_sem,
):
    frame = lax.axis_index("frame")
    patch = lax.axis_index("patch")
    y = patch // 4
    z = (patch // 2) % 2
    core = patch % 2
    sibling = (frame, y * 4 + z * 2 + (1 - core))
    across = (frame, y * 4 + (1 - z) * 2 + core)

    def along(step):
        return (frame, ((y + step) % 4) * 4 + z * 2 + core)

    loads = [pltpu.make_async_copy(tok.at[y], x.at[0, 0, 0], load_sem.at[0])]
    for part in range(3):
        columns = pl.ds(pl.multiple_of(part * D + core * 512, 128), WIN)
        loads.append(
            pltpu.make_async_copy(w_in.at[:, columns], w.at[:, pl.ds(part * WIN, WIN)], load_sem.at[1 + part])
        )
    loads.append(pltpu.make_async_copy(w_out, wo, load_sem.at[4]))
    for load in loads:
        load.start()

    barrier = pltpu.get_barrier_semaphore()
    for peer in (sibling, across, along(1), along(2), along(3)):
        pl.semaphore_signal(barrier, inc=1, device_id=peer, device_id_type=MESH)
    pl.semaphore_wait(barrier, 5)

    def remote(src, dst, send, recv, peer):
        return pltpu.make_async_remote_copy(
            src_ref=src, dst_ref=dst, send_sem=send, recv_sem=recv, device_id=peer, device_id_type=MESH
        )

    along_y = {}
    for d in (1, 3, 2):
        along_y[d] = remote(tok.at[(y + 4 - d) % 4], x.at[0, d, 0], y_send.at[d], y_recv.at[d], along(4 - d))
        along_y[d].start()
    loads[0].wait()

    to_sibling = {}
    over_z = {}

    def pass_on(d):
        over_z[d] = remote(x.at[0, d, 0], x.at[1, d, 0], z_send.at[d], z_recv.at[d], across)
        over_z[d].start()
        to_sibling[0, d] = remote(x.at[0, d, 0], x.at[0, d, 1], s_send.at[0, d], s_recv.at[0, d], sibling)
        to_sibling[0, d].start()

    def pass_z(d):
        over_z[d].wait_recv()
        to_sibling[1, d] = remote(x.at[1, d, 0], x.at[1, d, 1], s_send.at[1, d], s_recv.at[1, d], sibling)
        to_sibling[1, d].start()

    table = mod[0]

    def project(half, d):
        mixed = modulate(x[half, d].reshape(192, D), table)
        rows = pl.ds((half * 4 + d) * 192, 192)
        if half == 0:
            q[pl.ds(d * 192, 192), :] = (nn_dot(mixed, w[:, :WIN]) * SCALE).astype(jnp.bfloat16)
        k[rows, :] = nn_dot(mixed, w[:, WIN : 2 * WIN]).astype(jnp.bfloat16)
        v[rows, :] = nn_dot(mixed, w[:, 2 * WIN :]).astype(jnp.bfloat16)

    for step, d in enumerate(ORDER):
        if d:
            along_y[d].wait_recv()
        pass_on(d)
        to_sibling[0, d].wait_recv()
        if step == 0:
            for load in loads[1:4]:
                load.wait()
        project(0, d)
    for d in ORDER:
        pass_z(d)
        to_sibling[1, d].wait_recv()
        project(1, d)
    loads[4].wait()

    def attend(d):
        rows = pl.ds(d * 192, 192)
        carry = jnp.zeros((192, 128), jnp.float32)
        for j in range(4):
            window = slice(128 * j, 128 * j + 256)
            queries, keys, values = q[rows, window], k[:, window], v[:, window]
            both = head_attention(queries, keys, values, 16 * j + 64 * core, 255)
            both = both + head_attention(queries, keys, values, 16 * j + 72 + 64 * core, 0)
            att[d, :, 128 * j : 128 * j + 128] = (carry + both[:, :128]).astype(jnp.bfloat16)
            carry = both[:, 128:]
        att[d, :, 512:] = carry.astype(jnp.bfloat16)
        swap(d).start()

    def swap(d):
        return remote(att.at[d, pl.ds(96, 96)], att_in.at[d], a_send.at[d], a_recv.at[d], sibling)

    def give_back(d):
        return remote(u.at[d], out.at[y], r_send.at[d], r_recv.at[d], along(d))

    def finish(d):
        swap(d).wait_recv()
        mine = pl.ds(pl.multiple_of(core * 512, 128), WIN)
        other = pl.ds(pl.multiple_of((1 - core) * 512, 128), WIN)
        flat = nn_dot(att[d, :96], wo[mine, :]) + nn_dot(att_in[d], wo[other, :])
        u[d] = (x[0, d, 0].astype(jnp.float32) + table[2:3] * flat).astype(jnp.bfloat16)

    attend(1)

    def turn(d, carry):
        attend(d)
        finish(d - 1)
        give_back(d - 1).start()
        return carry

    lax.fori_loop(2, 4, turn, 0)
    attend(0)
    finish(3)
    give_back(3).start()
    finish(0)
    own = pltpu.make_async_copy(u.at[0], out.at[y], o_sem)
    own.start()

    for d in (1, 2, 3):
        landed = remote(u.at[d], out.at[(y + 4 - d) % 4], r_send.at[d], r_recv.at[d], along(d))
        landed.wait_recv()
        give_back(d).wait_send()
        along_y[d].wait_send()
    for d in range(4):
        swap(d).wait_send()
        over_z[d].wait_send()
        to_sibling[0, d].wait_send()
        to_sibling[1, d].wait_send()
    own.wait()


def spatial(tokens, modulation, w_in, w_out):
    dma = pltpu.SemaphoreType.DMA
    any_space = pl.BlockSpec(memory_space=pl.ANY)
    return pl.pallas_call(
        spatial_kernel,
        out_shape=jax.ShapeDtypeStruct((4, 96, D), jnp.bfloat16),
        in_specs=[any_space, pl.BlockSpec(memory_space=pltpu.VMEM), any_space, any_space],
        out_specs=any_space,
        scratch_shapes=[
            pltpu.VMEM((2, 4, 2, 96, D), jnp.bfloat16),
            pltpu.VMEM((D, 3 * WIN), jnp.bfloat16),
            pltpu.VMEM((D, D), jnp.bfloat16),
            pltpu.VMEM((768, WIN), jnp.bfloat16),
            pltpu.VMEM((1536, WIN), jnp.bfloat16),
            pltpu.VMEM((1536, WIN), jnp.bfloat16),
            pltpu.VMEM((4, 192, WIN), jnp.bfloat16),
            pltpu.VMEM((4, 96, WIN), jnp.bfloat16),
            pltpu.VMEM((4, 96, D), jnp.bfloat16),
            dma((5,)),
            dma((4,)), dma((4,)),
            dma((2, 4)), dma((2, 4)),
            dma((4,)), dma((4,)),
            dma((4,)), dma((4,)),
            dma((4,)), dma((4,)),
            dma,
        ],
        compiler_params=pltpu.CompilerParams(
            collective_id=0, has_side_effects=True, vmem_limit_bytes=VMEM_LIMIT
        ),
        name="spatial_block",
    )(tokens, modulation, w_in, w_out)


def shuffle(rows_to, forward):
    a = lax.broadcasted_iota(jnp.int32, (384, 384), 0)
    b = lax.broadcasted_iota(jnp.int32, (384, 384), 1)
    grouped, plain = (a, b) if forward else (b, a)
    source = ((grouped // 4) % 4) * 96 + (grouped // 16) * 4 + grouped % 4
    return jnp.where(source == plain, 1.0, 0.0).astype(jnp.bfloat16)


def temporal_kernel(
    upd, mod, w_in, w_out, out,
    w, wo, g, t, packed, att, r, back,
    load_sem, g_send, g_recv, r_send, r_recv, own_sem,
):
    frame = lax.axis_index("frame")
    patch = lax.axis_index("patch")
    loads = [pltpu.make_async_copy(w_in, w, load_sem.at[0]), pltpu.make_async_copy(w_out, wo, load_sem.at[1])]
    for load in loads:
        load.start()

    def peer(step):
        return ((frame + step) % 8, patch)

    barrier = pltpu.get_barrier_semaphore()
    for step in range(1, 8):
        pl.semaphore_signal(barrier, inc=1, device_id=peer(step), device_id_type=MESH)

    g[...] = nn_dot(shuffle(384, True), upd[...].reshape(384, D)).astype(jnp.bfloat16).reshape(8, 3, 16, D)
    pl.semaphore_wait(barrier, 7)

    def remote(src, dst, send, recv, device):
        return pltpu.make_async_remote_copy(
            src_ref=src, dst_ref=dst, send_sem=send, recv_sem=recv, device_id=device, device_id_type=MESH
        )

    def spread(step):
        return remote(g.at[(frame + step) % 8], t.at[:, frame], g_send.at[step], g_recv.at[step], peer(step))

    def spread_in(step):
        return remote(g.at[0], t.at[:, (frame + 8 - step) % 8], g_send.at[step], g_recv.at[step], peer(step))

    def collect(step):
        return remote(r.at[:, (frame + step) % 8], back.at[frame], r_send.at[step], r_recv.at[step], peer(step))

    def collect_in(step):
        return remote(r.at[:, 0], back.at[(frame + 8 - step) % 8], r_send.at[step], r_recv.at[step], peer(step))

    for step in range(1, 8):
        spread(step).start()
    own = pltpu.make_async_copy(g.at[frame], t.at[:, frame], own_sem.at[0])
    own.start()
    own.wait()
    for step in range(1, 8):
        spread_in(step).wait_recv()

    table = mod[1]
    loads[0].wait()
    mixed = modulate(t[...].reshape(384, D), table)
    packed[:, :D] = (nn_dot(mixed, w[:, :D]) * SCALE).astype(jnp.bfloat16)
    packed[:, D : 2 * D] = nn_dot(mixed, w[:, D : 2 * D]).astype(jnp.bfloat16)
    packed[:, 2 * D :] = nn_dot(mixed, w[:, 2 * D :]).astype(jnp.bfloat16)

    a = lax.broadcasted_iota(jnp.int32, (128, 128), 0)
    b = lax.broadcasted_iota(jnp.int32, (128, 128), 1)
    bias = jnp.where(a % 4 == b % 4, 0.0, -1e30)

    def attend(group, carry):
        rows = pl.ds(pl.multiple_of(group * 128, 128), 128)
        tiles = {}
        for h in range(HEADS):
            tile = min(HEAD * h // 128, 7)
            start = HEAD * h - 128 * tile
            at = 128 * tile
            mixed = head_attention(
                packed[rows, at : at + 256],
                packed[rows, D + at : D + at + 256],
                packed[rows, 2 * D + at : 2 * D + at + 256],
                start, 0 if start else 255, bias,
            )
            for side in range(2):
                piece = mixed[:, 128 * side : 128 * side + 128]
                tiles[tile + side] = tiles[tile + side] + piece if tile + side in tiles else piece
        for tile in range(9):
            att[rows, 128 * tile : 128 * tile + 128] = tiles[tile].astype(jnp.bfloat16)
        return carry

    lax.fori_loop(0, 3, attend, 0)
    loads[1].wait()
    flat = nn_dot(att[...], wo[...])
    r[...] = (
        (t[...].reshape(384, D).astype(jnp.float32) + table[2:3] * flat).astype(jnp.bfloat16).reshape(3, 8, 16, D)
    )
    for step in range(1, 8):
        collect(step).start()
    own = pltpu.make_async_copy(r.at[:, frame], back.at[frame], own_sem.at[1])
    own.start()
    own.wait()
    for step in range(1, 8):
        collect_in(step).wait_recv()
    out[...] = nn_dot(shuffle(384, False), back[...].reshape(384, D)).astype(jnp.bfloat16).reshape(4, 96, D)
    for step in range(1, 8):
        spread(step).wait_send()
        collect(step).wait_send()


def temporal(updated, modulation, w_in, w_out):
    dma = pltpu.SemaphoreType.DMA
    any_space = pl.BlockSpec(memory_space=pl.ANY)
    vmem = pl.BlockSpec(memory_space=pltpu.VMEM)
    return pl.pallas_call(
        temporal_kernel,
        out_shape=jax.ShapeDtypeStruct((4, 96, D), jnp.bfloat16),
        in_specs=[vmem, vmem, any_space, any_space],
        out_specs=vmem,
        scratch_shapes=[
            pltpu.VMEM((D, 3 * D), jnp.bfloat16),
            pltpu.VMEM((D, D), jnp.bfloat16),
            pltpu.VMEM((8, 3, 16, D), jnp.bfloat16),
            pltpu.VMEM((3, 8, 16, D), jnp.bfloat16),
            pltpu.VMEM((384, 3 * D), jnp.bfloat16),
            pltpu.VMEM((384, D), jnp.bfloat16),
            pltpu.VMEM((3, 8, 16, D), jnp.bfloat16),
            pltpu.VMEM((8, 3, 16, D), jnp.bfloat16),
            dma((2,)),
            dma((8,)), dma((8,)),
            dma((8,)), dma((8,)),
            dma((2,)),
        ],
        compiler_params=pltpu.CompilerParams(
            collective_id=1, has_side_effects=True, vmem_limit_bytes=VMEM_LIMIT
        ),
        name="temporal_block",
    )(updated, modulation, w_in, w_out)


def shards(tokens, modulation, spatial_input, spatial_output, temporal_input, temporal_output):
    updated = spatial(tokens, modulation, spatial_input, spatial_output)
    return temporal(updated, modulation, temporal_input, temporal_output)


def solution(mesh):
    in_specs = (P("frame", "patch", None), P(), P(), P(), P(), P())
    out_specs = P("frame", "patch", None)
    return jax.shard_map(shards, mesh=mesh, in_specs=in_specs, out_specs=out_specs, check_vma=False)
```

```python
import math

import jax
import jax.numpy as jnp
from jax import lax
from jax.experimental import pallas as pl
from jax.experimental.pallas import tpu as pltpu
from jax.sharding import PartitionSpec as P

D = 1152
HEADS = 16
HEAD = 72
WIN = 640
EARLY = 960
SCALE = math.log2(math.e) / math.sqrt(HEAD)
MESH = pl.DeviceIdType.MESH
VMEM_LIMIT = 60 * 1024 * 1024
STEPS = (0, 1, 3, 2)


def modulate(values, table):
    wide = values.astype(jnp.float32)
    centre = jnp.mean(wide, axis=-1, keepdims=True)
    wide = wide - centre
    spread = jnp.mean(jnp.square(wide), axis=-1, keepdims=True)
    normed = wide * lax.rsqrt(spread + 1e-06)
    return (normed * (1.0 + table[1]) + table[0]).astype(jnp.bfloat16)


def nt_dot(a, b):
    return lax.dot_general(a, b, (((1,), (1,)), ((), ())), preferred_element_type=jnp.float32)


def nn_dot(a, b):
    return jnp.dot(a, b, preferred_element_type=jnp.float32)


def lanes(width):
    return lax.broadcasted_iota(jnp.int32, (1, width), 1)


def head_lanes(start):
    return (lanes(256) >= start) & (lanes(256) < start + HEAD)


def choose(queries, mine):
    return queries * jnp.where(mine, 1.0, 0.0).astype(jnp.bfloat16)


def count_in(values, free):
    one = jnp.where(lanes(256) == free, 1.0, 0.0)
    return values * (1.0 - one).astype(jnp.bfloat16) + one.astype(jnp.bfloat16)


def shuffle(forward):
    a = lax.broadcasted_iota(jnp.int32, (128, 128), 0)
    b = lax.broadcasted_iota(jnp.int32, (128, 128), 1)
    grouped, plain = (a, b) if forward else (b, a)
    source = ((grouped // 4) % 4) * 32 + (grouped // 16) * 4 + grouped % 4
    return jnp.where(source == plain, 1.0, 0.0).astype(jnp.bfloat16)


def kernel(
    tok, mod, w_in0, w_out0, w_in1, w_out1, out,
    x, w, wo, q, k, v, first, stat, att, att_in, u, gathered,
    wt, wto, grouped, t, packed, mixed_t, r, back, res,
    load_sem, y_send, y_recv, s_send, s_recv, z_send, z_recv, a_send, a_recv,
    u_send, u_recv, g_send, g_recv, r_send, r_recv, own_sem, o_sem,
):
    frame = lax.axis_index("frame")
    patch = lax.axis_index("patch")
    y = patch // 4
    z = (patch // 2) % 2
    core = patch % 2
    sibling = (frame, y * 4 + z * 2 + (1 - core))
    across = (frame, y * 4 + (1 - z) * 2 + core)

    def along(step):
        return (frame, ((y + step) % 4) * 4 + z * 2 + core)

    def peer(step):
        return ((frame + step) % 8, patch)

    loads = [pltpu.make_async_copy(tok.at[y], x.at[0, 0, 0], load_sem.at[0])]
    for part in range(3):
        columns = pl.ds(pl.multiple_of(part * D + core * 512, 128), WIN)
        loads.append(
            pltpu.make_async_copy(w_in0.at[:, columns], w.at[:, pl.ds(part * WIN, WIN)], load_sem.at[1 + part])
        )
    loads.append(pltpu.make_async_copy(w_out0, wo, load_sem.at[4]))
    loads.append(pltpu.make_async_copy(w_in1, wt, load_sem.at[5]))
    loads.append(pltpu.make_async_copy(w_out1, wto, load_sem.at[6]))
    for load in loads:
        load.start()

    barrier = pltpu.get_barrier_semaphore()
    greeted = [sibling, across] + [along(s) for s in (1, 2, 3)] + [peer(s) for s in range(1, 8)]
    for device in greeted:
        pl.semaphore_signal(barrier, inc=1, device_id=device, device_id_type=MESH)
    pl.semaphore_wait(barrier, len(greeted))

    def remote(src, dst, send, recv, device):
        return pltpu.make_async_remote_copy(
            src_ref=src, dst_ref=dst, send_sem=send, recv_sem=recv, device_id=device, device_id_type=MESH
        )

    def along_y(slot):
        step = STEPS[slot]
        return remote(tok.at[(y + 4 - step) % 4], x.at[0, slot, 0], y_send.at[slot], y_recv.at[slot], along(4 - step))

    def over_z(slot):
        return remote(x.at[0, slot, 0], x.at[1, slot, 0], z_send.at[slot], z_recv.at[slot], across)

    def to_sibling(half, slot):
        return remote(x.at[half, slot, 0], x.at[half, slot, 1], s_send.at[half, slot], s_recv.at[half, slot], sibling)

    def pass_on(slot):
        over_z(slot).start()
        to_sibling(0, slot).start()

    def pass_z(slot):
        over_z(slot).wait_recv()
        to_sibling(1, slot).start()

    table = [mod[part, 0:1, :] for part in range(3)]

    def project(half, slot):
        to_sibling(half, slot).wait_recv()
        mixed = modulate(x[half, slot].reshape(192, D), table)
        rows = pl.ds((half * 4 + slot) * 192, 192)
        if half == 0:
            queries = (nn_dot(mixed, w[:, :WIN]) * SCALE).astype(jnp.bfloat16)
            for quarter in range(2):
                for g in range(3):
                    q[pl.ds(g * 256 + quarter * 128 + slot * 32, 32), :] = queries[
                        quarter * 96 + g * 32 : quarter * 96 + g * 32 + 32
                    ]
        k[rows, :] = nn_dot(mixed, w[:, WIN : 2 * WIN]).astype(jnp.bfloat16)
        v[rows, :] = nn_dot(mixed, w[:, 2 * WIN :]).astype(jnp.bfloat16)

    along_y(1).start()
    along_y(2).start()
    loads[0].wait()
    pass_on(0)
    along_y(1).wait_send()
    along_y(3).start()
    for load in loads[1:4]:
        load.wait()
    project(0, 0)
    along_y(1).wait_recv()
    pass_on(1)
    along_y(2).wait_recv()
    pass_on(2)
    pass_z(0)
    project(0, 1)
    project(0, 2)
    along_y(3).wait_recv()
    pass_on(3)
    project(1, 0)
    project(0, 3)

    def starts(j):
        return ((16 * j + 64 * core, 255), (16 * j + 72 + 64 * core, 0))

    def early(g, carry):
        @pl.when(g > 0)
        def _():
            pass_z(g)

        rows = pl.ds(pl.multiple_of(g * 256, 256), 256)
        held = jnp.zeros((256, 128), jnp.float32)
        for j in range(4):
            window = slice(128 * j, 128 * j + 256)
            queries, keys, values = q[rows, window], k[:EARLY, window], v[:EARLY, window]
            both = jnp.zeros((256, 256), jnp.float32)
            for odd, (start, free) in enumerate(starts(j)):
                mine = head_lanes(start)
                scores = nt_dot(choose(queries, mine), keys)
                top = jnp.max(scores, axis=-1, keepdims=True)
                weights = jnp.exp2(scores - top).astype(jnp.bfloat16)
                part = nn_dot(weights, count_in(values, free))
                both = jnp.where(mine, part, both)
                held = jnp.where(lanes(128) == 2 * j + odd, top, held)
                held = jnp.where(lanes(128) == 8 + 2 * j + odd, part[:, free : free + 1], held)
            first[j, rows] = both
        stat[rows] = held
        return carry

    def late(g, j, carry):
        rows = pl.ds(pl.multiple_of(g * 256, 256), 256)
        window = slice(128 * j, 128 * j + 256)
        queries, keys, values = q[rows, window], k[EARLY:, window], v[EARLY:, window]
        held = stat[rows]
        both = jnp.zeros((256, 256), jnp.float32)
        factor = jnp.zeros((256, 256), jnp.float32)
        for odd, (start, free) in enumerate(starts(j)):
            mine = head_lanes(start)
            scores = nt_dot(choose(queries, mine), keys)
            before = held[:, 2 * j + odd : 2 * j + odd + 1]
            top = jnp.maximum(before, jnp.max(scores, axis=-1, keepdims=True))
            weights = jnp.exp2(scores - top).astype(jnp.bfloat16)
            part = nn_dot(weights, count_in(values, free))
            shrink = jnp.exp2(before - top)
            share = 1.0 / (held[:, 8 + 2 * j + odd : 9 + 2 * j + odd] * shrink + part[:, free : free + 1])
            both = jnp.where(mine, part * share, both)
            factor = jnp.where(mine, shrink * share, factor)
        both = both + first[j, rows] * factor
        att[g, :, 128 * j : 128 * j + 128] = (carry + both[:, :128]).astype(jnp.bfloat16)
        if j == 3:
            att[g, :, 512:] = both[:, 128:].astype(jnp.bfloat16)
        return both[:, 128:]

    def swap(g):
        return remote(att.at[g, pl.ds(128, 128)], att_in.at[g], a_send.at[g], a_recv.at[g], sibling)

    def give(g, slot):
        return remote(u.at[g, slot], gathered.at[g, y], u_send.at[g, slot], u_recv.at[g, slot], along(STEPS[slot]))

    def own_give(g):
        return pltpu.make_async_copy(u.at[g, 0], gathered.at[g, y], own_sem.at[0, g])

    def finish(g):
        swap(g).wait_recv()
        mine = pl.ds(pl.multiple_of(core * 512, 128), WIN)
        other = pl.ds(pl.multiple_of((1 - core) * 512, 128), WIN)
        flat = nn_dot(att[g, :128], wo[mine, :]) + nn_dot(att_in[g], wo[other, :])
        values = x[0, :, 0, pl.ds(pl.multiple_of(g * 32, 32), 32), :].astype(jnp.float32)
        u[g] = (values + table[2] * flat.reshape(4, 32, D)).astype(jnp.bfloat16)
        for slot in range(1, 4):
            give(g, slot).start()
        own_give(g).start()

    lax.fori_loop(0, 3, early, 0)
    project(1, 1)
    project(1, 2)
    pass_z(3)
    project(1, 3)
    loads[4].wait()

    def turn(g, carry):
        edge = jnp.zeros((256, 128), jnp.float32)
        edge = late(g, 0, edge)
        edge = late(g, 1, edge)

        @pl.when(g > 0)
        def _():
            finish(g - 1)

        edge = late(g, 2, edge)
        late(g, 3, edge)
        swap(g).start()
        return carry

    lax.fori_loop(0, 3, turn, 0)
    finish(2)

    def spread(g, step):
        return remote(
            grouped.at[g, (frame + step) % 8], t.at[g, frame], g_send.at[g, step], g_recv.at[g, step], peer(step)
        )

    def own_spread(g):
        return pltpu.make_async_copy(grouped.at[g, frame], t.at[g, frame], own_sem.at[1, g])

    def collect(g, step):
        return remote(r.at[g, (frame + step) % 8], back.at[g, frame], r_send.at[g, step], r_recv.at[g, step], peer(step))

    def own_collect(g):
        return pltpu.make_async_copy(r.at[g, frame], back.at[g, frame], own_sem.at[2, g])

    forward = shuffle(True)

    def relay(g, carry):
        own_give(g).wait()
        for slot in range(1, 4):
            give(g, slot).wait_recv()
        grouped[g] = nn_dot(forward, gathered[g].reshape(128, D)).astype(jnp.bfloat16).reshape(8, 16, D)
        for step in range(1, 8):
            spread(g, step).start()
        own_spread(g).start()
        return carry

    lax.fori_loop(0, 3, relay, 0)
    loads[5].wait()
    loads[6].wait()

    a = lax.broadcasted_iota(jnp.int32, (128, 128), 0)
    b = lax.broadcasted_iota(jnp.int32, (128, 128), 1)
    bias = jnp.where(a % 4 == b % 4, 0.0, -1e30)
    table1 = [mod[part, 1:2, :] for part in range(3)]

    def block(g, carry):
        own_spread(g).wait()
        for step in range(1, 8):
            spread(g, step).wait_recv()
        values = t[g].reshape(128, D)
        mixed = modulate(values, table1)
        packed[:, :D] = (nn_dot(mixed, wt[:, :D]) * SCALE).astype(jnp.bfloat16)
        packed[:, D : 2 * D] = nn_dot(mixed, wt[:, D : 2 * D]).astype(jnp.bfloat16)
        packed[:, 2 * D :] = nn_dot(mixed, wt[:, 2 * D :]).astype(jnp.bfloat16)
        spots = []
        scores = []
        for h in range(HEADS):
            at = 128 * min(HEAD * h // 128, 7)
            start = HEAD * h - at
            spots.append((at, head_lanes(start), 0 if start else 255))
            queries = choose(packed[:, at : at + 256], spots[h][1])
            scores.append(nt_dot(queries, packed[:, D + at : D + at + 256]) + bias)
        weights = []
        for h in range(HEADS):
            top = jnp.max(scores[h], axis=-1, keepdims=True)
            weights.append(jnp.exp2(scores[h] - top).astype(jnp.bfloat16))
        tiles = [None] * 9
        for h, (at, mine, free) in enumerate(spots):
            part = nn_dot(weights[h], count_in(packed[:, 2 * D + at : 2 * D + at + 256], free))
            part = jnp.where(mine, part * (1.0 / part[:, free : free + 1]), 0.0)
            for side in range(2):
                tile = at // 128 + side
                piece = part[:, 128 * side : 128 * side + 128]
                tiles[tile] = piece if tiles[tile] is None else tiles[tile] + piece
        for tile in range(9):
            mixed_t[:, 128 * tile : 128 * tile + 128] = tiles[tile].astype(jnp.bfloat16)
        flat = nn_dot(mixed_t[...], wto[...])
        r[g] = (values.astype(jnp.float32) + table1[2] * flat).astype(jnp.bfloat16).reshape(8, 16, D)
        for step in range(1, 8):
            collect(g, step).start()
        own_collect(g).start()
        return carry

    lax.fori_loop(0, 3, block, 0)

    backward = shuffle(False)

    def put(g):
        return pltpu.make_async_copy(res.at[g], out.at[:, pl.ds(pl.multiple_of(g * 32, 32), 32), :], o_sem.at[g])

    def settle(g, carry):
        own_collect(g).wait()
        for step in range(1, 8):
            collect(g, step).wait_recv()
        res[g] = nn_dot(backward, back[g].reshape(128, D)).astype(jnp.bfloat16).reshape(4, 32, D)
        put(g).start()
        return carry

    lax.fori_loop(0, 3, settle, 0)

    along_y(2).wait_send()
    along_y(3).wait_send()
    for slot in range(4):
        over_z(slot).wait_send()
        to_sibling(0, slot).wait_send()
        to_sibling(1, slot).wait_send()

    def drain(g, carry):
        swap(g).wait_send()
        for slot in range(1, 4):
            give(g, slot).wait_send()
        for step in range(1, 8):
            spread(g, step).wait_send()
            collect(g, step).wait_send()
        put(g).wait()
        return carry

    lax.fori_loop(0, 3, drain, 0)


def shards(tokens, modulation, spatial_input, spatial_output, temporal_input, temporal_output):
    dma = pltpu.SemaphoreType.DMA
    held = pl.BlockSpec(memory_space=pl.ANY)

    def bf16(*shape):
        return pltpu.VMEM(shape, jnp.bfloat16)

    return pl.pallas_call(
        kernel,
        out_shape=jax.ShapeDtypeStruct((4, 96, D), jnp.bfloat16),
        in_specs=[held, pl.BlockSpec(memory_space=pltpu.VMEM), held, held, held, held],
        out_specs=held,
        scratch_shapes=[
            bf16(2, 4, 2, 96, D),
            bf16(D, 3 * WIN),
            bf16(D, D),
            bf16(768, WIN),
            bf16(1536, WIN),
            bf16(1536, WIN),
            pltpu.VMEM((4, 768, 256), jnp.float32),
            pltpu.VMEM((768, 128), jnp.float32),
            bf16(3, 256, WIN),
            bf16(3, 128, WIN),
            bf16(3, 4, 32, D),
            bf16(3, 4, 32, D),
            bf16(D, 3 * D),
            bf16(D, D),
            bf16(3, 8, 16, D),
            bf16(3, 8, 16, D),
            bf16(128, 3 * D),
            bf16(128, D),
            bf16(3, 8, 16, D),
            bf16(3, 8, 16, D),
            bf16(3, 4, 32, D),
            dma((7,)),
            dma((4,)), dma((4,)),
            dma((2, 4)), dma((2, 4)),
            dma((4,)), dma((4,)),
            dma((3,)), dma((3,)),
            dma((3, 4)), dma((3, 4)),
            dma((3, 8)), dma((3, 8)),
            dma((3, 8)), dma((3, 8)),
            dma((3, 3)),
            dma((3,)),
        ],
        compiler_params=pltpu.CompilerParams(
            collective_id=0, has_side_effects=True, vmem_limit_bytes=VMEM_LIMIT
        ),
        name="block_pair",
    )(tokens, jnp.transpose(modulation, (1, 0, 2)), spatial_input, spatial_output, temporal_input, temporal_output)


def solution(mesh):
    in_specs = (P("frame", "patch", None), P(), P(), P(), P(), P())
    out_specs = P("frame", "patch", None)
    return jax.shard_map(shards, mesh=mesh, in_specs=in_specs, out_specs=out_specs, check_vma=False)
```

```python
import math

import jax
import jax.numpy as jnp
from jax import lax
from jax.experimental import pallas as pl
from jax.experimental.pallas import tpu as pltpu
from jax.sharding import PartitionSpec as P

D = 1152
HEADS = 16
HEAD = 72
WIN = 640
EARLY = 1152
LATE = 384
SCALE = math.log2(math.e) / math.sqrt(HEAD)
MESH = pl.DeviceIdType.MESH
VMEM_LIMIT = 60 * 1024 * 1024
STEPS = (0, 1, 3, 2)


def modulate(values, table):
    wide = values.astype(jnp.float32)
    centre = jnp.mean(wide, axis=-1, keepdims=True)
    wide = wide - centre
    spread = jnp.mean(jnp.square(wide), axis=-1, keepdims=True)
    normed = wide * lax.rsqrt(spread + 1e-06)
    return (normed * (1.0 + table[1]) + table[0]).astype(jnp.bfloat16)


def nt_dot(a, b):
    return lax.dot_general(a, b, (((1,), (1,)), ((), ())), preferred_element_type=jnp.float32)


def nn_dot(a, b):
    return jnp.dot(a, b, preferred_element_type=jnp.float32)


def lanes(width):
    return lax.broadcasted_iota(jnp.int32, (1, width), 1)


def head_lanes(start):
    return (lanes(256) >= start) & (lanes(256) < start + HEAD)


def choose(queries, mine):
    return queries * jnp.where(mine, 1.0, 0.0).astype(jnp.bfloat16)


def count_in(values, free):
    one = jnp.where(lanes(256) == free, 1.0, 0.0)
    return values * (1.0 - one).astype(jnp.bfloat16) + one.astype(jnp.bfloat16)


def shuffle(forward):
    a = lax.broadcasted_iota(jnp.int32, (128, 128), 0)
    b = lax.broadcasted_iota(jnp.int32, (128, 128), 1)
    grouped, plain = (a, b) if forward else (b, a)
    source = ((grouped // 4) % 4) * 32 + (grouped // 16) * 4 + grouped % 4
    return jnp.where(source == plain, 1.0, 0.0).astype(jnp.bfloat16)


def kernel(
    tok, mod, w_in0, w_out0, w_in1, w_out1, out,
    x, w, wo, q, k, v, first, stat, att, att_in, u, gathered,
    wt, wto, grouped, t, packed, mixed_t, r, back, res,
    load_sem, y_send, y_recv, s_send, s_recv, z_send, z_recv, a_send, a_recv,
    u_send, u_recv, g_send, g_recv, r_send, r_recv, own_sem, o_sem, meet_sem,
):
    frame = lax.axis_index("frame")
    patch = lax.axis_index("patch")
    y = patch // 4
    z = (patch // 2) % 2
    core = patch % 2
    sibling = (frame, y * 4 + z * 2 + (1 - core))
    across = (frame, y * 4 + (1 - z) * 2 + core)

    def along(step):
        return (frame, ((y + step) % 4) * 4 + z * 2 + core)

    def peer(step):
        return ((frame + step) % 8, patch)

    def beside_x(step):
        return ((frame // 4) * 4 + (frame + step) % 4, patch)

    opposite = ((frame + 4) % 8, patch)
    over_edge = ((frame + 4) % 8, y * 4 + (1 - z) * 2 + core)

    loads = [pltpu.make_async_copy(tok.at[y], x.at[0, 0, 0], load_sem.at[0])]
    for part in range(3):
        columns = pl.ds(pl.multiple_of(part * D + core * 512, 128), WIN)
        loads.append(
            pltpu.make_async_copy(w_in0.at[:, columns], w.at[:, pl.ds(part * WIN, WIN)], load_sem.at[1 + part])
        )
    loads.append(pltpu.make_async_copy(w_out0, wo, load_sem.at[4]))
    loads.append(pltpu.make_async_copy(w_in1, wt, load_sem.at[5]))
    loads.append(pltpu.make_async_copy(w_out1, wto, load_sem.at[6]))
    for load in loads[:4]:
        load.start()

    barrier = pltpu.get_barrier_semaphore()
    beside = [beside_x(1), beside_x(3)]
    greeted = [sibling, across] + [along(s) for s in (1, 2, 3)] + beside + [over_edge]
    for device in greeted:
        pl.semaphore_signal(barrier, inc=1, device_id=device, device_id_type=MESH)
    pl.semaphore_wait(barrier, len(greeted))

    for device in beside + [across]:
        pl.semaphore_signal(meet_sem.at[0], inc=1, device_id=device, device_id_type=MESH)

    def remote(src, dst, send, recv, device):
        return pltpu.make_async_remote_copy(
            src_ref=src, dst_ref=dst, send_sem=send, recv_sem=recv, device_id=device, device_id_type=MESH
        )

    def along_y(slot):
        step = STEPS[slot]
        return remote(tok.at[(y + 4 - step) % 4], x.at[0, slot, 0], y_send.at[slot], y_recv.at[slot], along(4 - step))

    def over_z(slot):
        return remote(x.at[0, slot, 0], x.at[1, slot, 0], z_send.at[slot], z_recv.at[slot], across)

    def to_sibling(half, slot):
        return remote(x.at[half, slot, 0], x.at[half, slot, 1], s_send.at[half, slot], s_recv.at[half, slot], sibling)

    def pass_on(slot):
        over_z(slot).start()
        to_sibling(0, slot).start()

    def pass_z(slot):
        over_z(slot).wait_recv()
        to_sibling(1, slot).start()

    table = [mod[part, 0:1, :] for part in range(3)]

    def project(half, slot):
        to_sibling(half, slot).wait_recv()
        mixed = modulate(x[half, slot].reshape(192, D), table)
        rows = pl.ds((half * 4 + slot) * 192, 192)
        if half == 0:
            queries = (nn_dot(mixed, w[:, :WIN]) * SCALE).astype(jnp.bfloat16)
            for quarter in range(2):
                for g in range(3):
                    q[pl.ds(g * 256 + quarter * 128 + slot * 32, 32), :] = queries[
                        quarter * 96 + g * 32 : quarter * 96 + g * 32 + 32
                    ]
        k[rows, :] = nn_dot(mixed, w[:, WIN : 2 * WIN]).astype(jnp.bfloat16)
        v[rows, :] = nn_dot(mixed, w[:, 2 * WIN :]).astype(jnp.bfloat16)

    along_y(1).start()
    along_y(2).start()
    loads[0].wait()
    pass_on(0)
    along_y(1).wait_send()
    along_y(3).start()
    for load in loads[1:4]:
        load.wait()
    for load in loads[4:]:
        load.start()
    project(0, 0)
    pl.semaphore_wait(meet_sem.at[0], 3)
    pl.semaphore_signal(meet_sem.at[1], inc=1, device_id=opposite, device_id_type=MESH)
    along_y(1).wait_recv()
    pass_on(1)
    along_y(2).wait_recv()
    pass_on(2)
    pass_z(0)
    project(0, 1)
    project(0, 2)
    along_y(3).wait_recv()
    pass_on(3)
    project(1, 0)
    project(0, 3)
    pass_z(1)
    project(1, 1)

    def starts(j):
        return ((16 * j + 64 * core, 255), (16 * j + 72 + 64 * core, 0))

    def early(g, carry):
        @pl.when(g == 2)
        def _():
            pass_z(2)

        rows = pl.ds(pl.multiple_of(g * 256, 256), 256)
        for j in range(4):
            window = slice(128 * j, 128 * j + 256)
            queries, keys, values = q[rows, window], k[:EARLY, window], v[:EARLY, window]
            for odd, (start, free) in enumerate(starts(j)):
                scores = nt_dot(choose(queries, head_lanes(start)), keys)
                top = jnp.max(scores, axis=-1, keepdims=True)
                weights = jnp.exp2(scores - top).astype(jnp.bfloat16)
                first[2 * j + odd, rows] = nn_dot(weights, count_in(values, free))
                stat[2 * j + odd, rows] = jnp.broadcast_to(top, (256, 128))
        return carry

    def late(g, j, carry):
        rows = pl.ds(pl.multiple_of(g * 256, 256), 256)
        window = slice(128 * j, 128 * j + 256)
        queries, keys, values = q[rows, window], k[EARLY:, window], v[EARLY:, window]
        both = jnp.zeros((256, 256), jnp.float32)
        for odd, (start, free) in enumerate(starts(j)):
            h = 2 * j + odd
            mine = head_lanes(start)
            scores = nt_dot(choose(queries, mine), keys)
            parts = [scores[:, 128 * n : 128 * n + 128] for n in range(LATE // 128)]
            top = parts[0]
            for piece in parts[1:]:
                top = jnp.maximum(top, piece)
            before = stat[h, rows]
            top = jnp.maximum(before, jnp.max(top, axis=-1, keepdims=True))
            weights = jnp.concatenate([jnp.exp2(piece - top).astype(jnp.bfloat16) for piece in parts], axis=1)
            part = nn_dot(weights, count_in(values, free))
            shrink = jnp.exp2(before - top)
            earlier = first[h, rows]
            total = jnp.concatenate(
                [part[:, :128] + earlier[:, :128] * shrink, part[:, 128:] + earlier[:, 128:] * shrink], axis=1
            )
            both = jnp.where(mine, total * (1.0 / total[:, free : free + 1]), both)
        att[g, :, 128 * j : 128 * j + 128] = (carry + both[:, :128]).astype(jnp.bfloat16)
        if j == 3:
            att[g, :, 512:] = both[:, 128:].astype(jnp.bfloat16)
        return both[:, 128:]

    def swap(g):
        return remote(att.at[g, pl.ds(128, 128)], att_in.at[g], a_send.at[g], a_recv.at[g], sibling)

    def give(g, slot):
        return remote(u.at[g, slot], gathered.at[g, y], u_send.at[g, slot], u_recv.at[g, slot], along(STEPS[slot]))

    def own_give(g):
        return pltpu.make_async_copy(u.at[g, 0], gathered.at[g, y], own_sem.at[0, g])

    def finish(g):
        swap(g).wait_recv()
        mine = pl.ds(pl.multiple_of(core * 512, 128), WIN)
        other = pl.ds(pl.multiple_of((1 - core) * 512, 128), WIN)
        flat = nn_dot(att[g, :128], wo[mine, :]) + nn_dot(att_in[g], wo[other, :])
        values = x[0, :, 0, pl.ds(pl.multiple_of(g * 32, 32), 32), :].astype(jnp.float32)
        u[g] = (values + table[2] * flat.reshape(4, 32, D)).astype(jnp.bfloat16)
        for slot in range(1, 4):
            give(g, slot).start()
        own_give(g).start()

    lax.fori_loop(0, 3, early, 0)
    pass_z(3)
    project(1, 2)
    project(1, 3)
    loads[4].wait()

    def turn(g, carry):
        edge = jnp.zeros((256, 128), jnp.float32)
        edge = late(g, 0, edge)
        edge = late(g, 1, edge)

        @pl.when(g > 0)
        def _():
            finish(g - 1)

        edge = late(g, 2, edge)
        late(g, 3, edge)
        swap(g).start()
        return carry

    lax.fori_loop(0, 3, turn, 0)
    finish(2)

    def spread(g, step):
        return remote(
            grouped.at[g, (frame + step) % 8], t.at[g, frame], g_send.at[g, step], g_recv.at[g, step], peer(step)
        )

    def own_spread(g):
        return pltpu.make_async_copy(grouped.at[g, frame], t.at[g, frame], own_sem.at[1, g])

    def collect(g, step):
        return remote(r.at[g, (frame + step) % 8], back.at[g, frame], r_send.at[g, step], r_recv.at[g, step], peer(step))

    def own_collect(g):
        return pltpu.make_async_copy(r.at[g, frame], back.at[g, frame], own_sem.at[2, g])

    forward = shuffle(True)
    pl.semaphore_wait(meet_sem.at[1], 1)

    def relay(g, carry):
        own_give(g).wait()
        for slot in range(1, 4):
            give(g, slot).wait_recv()
        grouped[g] = nn_dot(forward, gathered[g].reshape(128, D)).astype(jnp.bfloat16).reshape(8, 16, D)
        for step in range(1, 8):
            spread(g, step).start()
        own_spread(g).start()
        return carry

    lax.fori_loop(0, 3, relay, 0)
    loads[5].wait()
    loads[6].wait()

    a = lax.broadcasted_iota(jnp.int32, (128, 128), 0)
    b = lax.broadcasted_iota(jnp.int32, (128, 128), 1)
    bias = jnp.where(a % 4 == b % 4, 0.0, -1e30)
    table1 = [mod[part, 1:2, :] for part in range(3)]

    def block(g, carry):
        own_spread(g).wait()
        for step in range(1, 8):
            spread(g, step).wait_recv()
        values = t[g].reshape(128, D)
        mixed = modulate(values, table1)
        packed[:, :D] = (nn_dot(mixed, wt[:, :D]) * SCALE).astype(jnp.bfloat16)
        packed[:, D : 2 * D] = nn_dot(mixed, wt[:, D : 2 * D]).astype(jnp.bfloat16)
        packed[:, 2 * D :] = nn_dot(mixed, wt[:, 2 * D :]).astype(jnp.bfloat16)
        spots = []
        scores = []
        for h in range(HEADS):
            at = 128 * min(HEAD * h // 128, 7)
            start = HEAD * h - at
            spots.append((at, head_lanes(start), 0 if start else 255))
            queries = choose(packed[:, at : at + 256], spots[h][1])
            scores.append(nt_dot(queries, packed[:, D + at : D + at + 256]) + bias)
        weights = []
        for h in range(HEADS):
            top = jnp.max(scores[h], axis=-1, keepdims=True)
            weights.append(jnp.exp2(scores[h] - top).astype(jnp.bfloat16))
        tiles = [None] * 9
        for h, (at, mine, free) in enumerate(spots):
            part = nn_dot(weights[h], count_in(packed[:, 2 * D + at : 2 * D + at + 256], free))
            part = jnp.where(mine, part * (1.0 / part[:, free : free + 1]), 0.0)
            for side in range(2):
                tile = at // 128 + side
                piece = part[:, 128 * side : 128 * side + 128]
                tiles[tile] = piece if tiles[tile] is None else tiles[tile] + piece
        for tile in range(9):
            mixed_t[:, 128 * tile : 128 * tile + 128] = tiles[tile].astype(jnp.bfloat16)
        flat = nn_dot(mixed_t[...], wto[...])
        r[g] = (values.astype(jnp.float32) + table1[2] * flat).astype(jnp.bfloat16).reshape(8, 16, D)
        for step in range(1, 8):
            collect(g, step).start()
        own_collect(g).start()
        return carry

    lax.fori_loop(0, 3, block, 0)

    backward = shuffle(False)

    def put(g):
        return pltpu.make_async_copy(res.at[g], out.at[:, pl.ds(pl.multiple_of(g * 32, 32), 32), :], o_sem.at[g])

    def settle(g, carry):
        own_collect(g).wait()
        for step in range(1, 8):
            collect(g, step).wait_recv()
        res[g] = nn_dot(backward, back[g].reshape(128, D)).astype(jnp.bfloat16).reshape(4, 32, D)
        put(g).start()
        return carry

    lax.fori_loop(0, 3, settle, 0)

    along_y(2).wait_send()
    along_y(3).wait_send()
    for slot in range(4):
        over_z(slot).wait_send()
        to_sibling(0, slot).wait_send()
        to_sibling(1, slot).wait_send()

    def drain(g, carry):
        swap(g).wait_send()
        for slot in range(1, 4):
            give(g, slot).wait_send()
        for step in range(1, 8):
            spread(g, step).wait_send()
            collect(g, step).wait_send()
        put(g).wait()
        return carry

    lax.fori_loop(0, 3, drain, 0)


def shards(tokens, modulation, spatial_input, spatial_output, temporal_input, temporal_output):
    dma = pltpu.SemaphoreType.DMA
    held = pl.BlockSpec(memory_space=pl.ANY)

    def bf16(*shape):
        return pltpu.VMEM(shape, jnp.bfloat16)

    return pl.pallas_call(
        kernel,
        out_shape=jax.ShapeDtypeStruct((4, 96, D), jnp.bfloat16),
        in_specs=[held, pl.BlockSpec(memory_space=pltpu.VMEM), held, held, held, held],
        out_specs=held,
        scratch_shapes=[
            bf16(2, 4, 2, 96, D),
            bf16(D, 3 * WIN),
            bf16(D, D),
            bf16(768, WIN),
            bf16(1536, WIN),
            bf16(1536, WIN),
            pltpu.VMEM((8, 768, 256), jnp.float32),
            pltpu.VMEM((8, 768, 128), jnp.float32),
            bf16(3, 256, WIN),
            bf16(3, 128, WIN),
            bf16(3, 4, 32, D),
            bf16(3, 4, 32, D),
            bf16(D, 3 * D),
            bf16(D, D),
            bf16(3, 8, 16, D),
            bf16(3, 8, 16, D),
            bf16(128, 3 * D),
            bf16(128, D),
            bf16(3, 8, 16, D),
            bf16(3, 8, 16, D),
            bf16(3, 4, 32, D),
            dma((7,)),
            dma((4,)), dma((4,)),
            dma((2, 4)), dma((2, 4)),
            dma((4,)), dma((4,)),
            dma((3,)), dma((3,)),
            dma((3, 4)), dma((3, 4)),
            dma((3, 8)), dma((3, 8)),
            dma((3, 8)), dma((3, 8)),
            dma((3, 3)),
            dma((3,)),
            pltpu.SemaphoreType.REGULAR((2,)),
        ],
        compiler_params=pltpu.CompilerParams(
            collective_id=0, has_side_effects=True, vmem_limit_bytes=VMEM_LIMIT
        ),
        name="block_pair",
    )(tokens, jnp.transpose(modulation, (1, 0, 2)), spatial_input, spatial_output, temporal_input, temporal_output)


def solution(mesh):
    in_specs = (P("frame", "patch", None), P(), P(), P(), P(), P())
    out_specs = P("frame", "patch", None)
    return jax.shard_map(shards, mesh=mesh, in_specs=in_specs, out_specs=out_specs, check_vma=False)
```

```python
import math

import jax
import jax.numpy as jnp
from jax import lax
from jax.experimental import pallas as pl
from jax.experimental.pallas import tpu as pltpu
from jax.sharding import PartitionSpec as P

D = 1152
HEADS = 16
HEAD = 72
WIN = 640
EARLY = 1152
LATE = 384
SCALE = math.log2(math.e) / math.sqrt(HEAD)
MESH = pl.DeviceIdType.MESH
VMEM_LIMIT = 60 * 1024 * 1024
STEPS = (0, 1, 3, 2)


def modulate(values, table):
    wide = values.astype(jnp.float32)
    centre = jnp.mean(wide, axis=-1, keepdims=True)
    wide = wide - centre
    spread = jnp.mean(jnp.square(wide), axis=-1, keepdims=True)
    normed = wide * lax.rsqrt(spread + 1e-06)
    return (normed * (1.0 + table[1]) + table[0]).astype(jnp.bfloat16)


def nt_dot(a, b):
    return lax.dot_general(a, b, (((1,), (1,)), ((), ())), preferred_element_type=jnp.float32)


def nn_dot(a, b):
    return jnp.dot(a, b, preferred_element_type=jnp.float32)


def lanes(width):
    return lax.broadcasted_iota(jnp.int32, (1, width), 1)


def head_lanes(start):
    return (lanes(256) >= start) & (lanes(256) < start + HEAD)


def choose(queries, mine):
    return queries * jnp.where(mine, 1.0, 0.0).astype(jnp.bfloat16)


def count_in(values, free):
    one = jnp.where(lanes(256) == free, 1.0, 0.0)
    return values * (1.0 - one).astype(jnp.bfloat16) + one.astype(jnp.bfloat16)


def shuffle(forward):
    a = lax.broadcasted_iota(jnp.int32, (128, 128), 0)
    b = lax.broadcasted_iota(jnp.int32, (128, 128), 1)
    grouped, plain = (a, b) if forward else (b, a)
    source = ((grouped // 4) % 4) * 32 + (grouped // 16) * 4 + grouped % 4
    return jnp.where(source == plain, 1.0, 0.0).astype(jnp.bfloat16)


def kernel(
    tok, mod, w_in0, w_out0, w_in1, w_out1, out,
    x, m, w, wo, q, k, v, first, stat, att, att_in, u, gathered,
    wt, wto, grouped, t, packed, mixed_t, r, back, res,
    load_sem, y_send, y_recv, s_send, s_recv, z_send, z_recv, a_send, a_recv,
    u_send, u_recv, g_send, g_recv, r_send, r_recv, own_sem, o_sem, meet_sem,
):
    frame = lax.axis_index("frame")
    patch = lax.axis_index("patch")
    y = patch // 4
    z = (patch // 2) % 2
    core = patch % 2
    sibling = (frame, y * 4 + z * 2 + (1 - core))
    across = (frame, y * 4 + (1 - z) * 2 + core)

    def along(step):
        return (frame, ((y + step) % 4) * 4 + z * 2 + core)

    def peer(step):
        return ((frame + step) % 8, patch)

    def beside_x(step):
        return ((frame // 4) * 4 + (frame + step) % 4, patch)

    opposite = ((frame + 4) % 8, patch)
    over_edge = ((frame + 4) % 8, y * 4 + (1 - z) * 2 + core)

    loads = [pltpu.make_async_copy(tok.at[y], x.at[0], load_sem.at[0])]
    for part in range(3):
        columns = pl.ds(pl.multiple_of(part * D + core * 512, 128), WIN)
        loads.append(
            pltpu.make_async_copy(w_in0.at[:, columns], w.at[:, pl.ds(part * WIN, WIN)], load_sem.at[1 + part])
        )
    loads.append(pltpu.make_async_copy(w_out0, wo, load_sem.at[4]))
    loads.append(pltpu.make_async_copy(w_in1, wt, load_sem.at[5]))
    loads.append(pltpu.make_async_copy(w_out1, wto, load_sem.at[6]))
    for load in loads[:4]:
        load.start()

    barrier = pltpu.get_barrier_semaphore()
    beside = [beside_x(1), beside_x(3)]
    greeted = [sibling, across] + [along(s) for s in (1, 2, 3)] + beside + [over_edge]
    for device in greeted:
        pl.semaphore_signal(barrier, inc=1, device_id=device, device_id_type=MESH)
    table = [mod[part, 0:1, :] for part in range(3)]
    loads[0].wait()
    m[0, 0, 0] = modulate(x[0], table)
    pl.semaphore_wait(barrier, len(greeted))

    for device in beside + [across]:
        pl.semaphore_signal(meet_sem.at[0], inc=1, device_id=device, device_id_type=MESH)

    def remote(src, dst, send, recv, device):
        return pltpu.make_async_remote_copy(
            src_ref=src, dst_ref=dst, send_sem=send, recv_sem=recv, device_id=device, device_id_type=MESH
        )

    def along_y(slot):
        step = STEPS[slot]
        return remote(tok.at[(y + 4 - step) % 4], x.at[slot], y_send.at[slot], y_recv.at[slot], along(4 - step))

    def over_z(slot):
        return remote(m.at[0, slot, 0], m.at[1, slot, 0], z_send.at[slot], z_recv.at[slot], across)

    def to_sibling(half, slot):
        return remote(m.at[half, slot, 0], m.at[half, slot, 1], s_send.at[half, slot], s_recv.at[half, slot], sibling)

    def pass_on(slot):
        if slot:
            along_y(slot).wait_recv()
            m[0, slot, 0] = modulate(x[slot], table)
        over_z(slot).start()
        to_sibling(0, slot).start()

    def pass_z(slot):
        over_z(slot).wait_recv()
        to_sibling(1, slot).start()

    def project(half, slot, count):
        for n in range(count):
            to_sibling(half, slot + n).wait_recv()
        mixed = m[half, slot : slot + count].reshape(192 * count, D)
        rows = pl.ds((half * 4 + slot) * 192, 192 * count)
        if half == 0:
            flat = nn_dot(mixed, w[...])
            queries = (flat[:, :WIN] * SCALE).astype(jnp.bfloat16)
            for n in range(count):
                for quarter in range(2):
                    for g in range(3):
                        at = n * 192 + quarter * 96 + g * 32
                        q[pl.ds(g * 256 + quarter * 128 + (slot + n) * 32, 32), :] = queries[at : at + 32]
            flat = flat[:, WIN:]
        else:
            flat = nn_dot(mixed, w[:, WIN:])
        k[rows, :] = flat[:, :WIN].astype(jnp.bfloat16)
        v[rows, :] = flat[:, WIN:].astype(jnp.bfloat16)

    along_y(1).start()
    along_y(2).start()
    pass_on(0)
    along_y(1).wait_send()
    along_y(3).start()
    for load in loads[1:4]:
        load.wait()
    for load in loads[4:]:
        load.start()
    project(0, 0, 1)
    pl.semaphore_wait(meet_sem.at[0], 3)
    pl.semaphore_signal(meet_sem.at[1], inc=1, device_id=opposite, device_id_type=MESH)
    pass_on(1)
    pass_on(2)
    pass_z(0)
    project(0, 1, 2)
    pass_on(3)
    project(0, 3, 1)
    pass_z(1)
    project(1, 0, 2)

    def starts(j):
        return ((16 * j + 64 * core, 255), (16 * j + 72 + 64 * core, 0))

    def early(g, carry):
        @pl.when(g == 2)
        def _():
            pass_z(2)

        rows = pl.ds(pl.multiple_of(g * 256, 256), 256)
        for j in range(4):
            window = slice(128 * j, 128 * j + 256)
            queries, keys, values = q[rows, window], k[:EARLY, window], v[:EARLY, window]
            for odd, (start, free) in enumerate(starts(j)):
                scores = nt_dot(choose(queries, head_lanes(start)), keys)
                top = jnp.max(scores, axis=-1, keepdims=True)
                weights = jnp.exp2(scores - top).astype(jnp.bfloat16)
                first[2 * j + odd, rows] = nn_dot(weights, count_in(values, free))
                stat[2 * j + odd, rows] = jnp.broadcast_to(top, (256, 128))
        return carry

    def late(g, j, carry):
        rows = pl.ds(pl.multiple_of(g * 256, 256), 256)
        window = slice(128 * j, 128 * j + 256)
        queries, keys, values = q[rows, window], k[EARLY:, window], v[EARLY:, window]
        both = jnp.zeros((256, 256), jnp.float32)
        for odd, (start, free) in enumerate(starts(j)):
            h = 2 * j + odd
            mine = head_lanes(start)
            scores = nt_dot(choose(queries, mine), keys)
            parts = [scores[:, 128 * n : 128 * n + 128] for n in range(LATE // 128)]
            top = parts[0]
            for piece in parts[1:]:
                top = jnp.maximum(top, piece)
            before = stat[h, rows]
            top = jnp.maximum(before, jnp.max(top, axis=-1, keepdims=True))
            weights = jnp.concatenate([jnp.exp2(piece - top).astype(jnp.bfloat16) for piece in parts], axis=1)
            part = nn_dot(weights, count_in(values, free))
            shrink = jnp.exp2(before - top)
            earlier = first[h, rows]
            total = jnp.concatenate(
                [part[:, :128] + earlier[:, :128] * shrink, part[:, 128:] + earlier[:, 128:] * shrink], axis=1
            )
            both = jnp.where(mine, total * (1.0 / total[:, free : free + 1]), both)
        att[g, :, 128 * j : 128 * j + 128] = (carry + both[:, :128]).astype(jnp.bfloat16)
        if j == 3:
            att[g, :, 512:] = both[:, 128:].astype(jnp.bfloat16)
        return both[:, 128:]

    def swap(g):
        return remote(att.at[g, pl.ds(128, 128)], att_in.at[g], a_send.at[g], a_recv.at[g], sibling)

    def give(g, slot):
        return remote(u.at[g, slot], gathered.at[g, y], u_send.at[g, slot], u_recv.at[g, slot], along(STEPS[slot]))

    def own_give(g):
        return pltpu.make_async_copy(u.at[g, 0], gathered.at[g, y], own_sem.at[0, g])

    def finish(g):
        swap(g).wait_recv()
        mine = pl.ds(pl.multiple_of(core * 512, 128), WIN)
        other = pl.ds(pl.multiple_of((1 - core) * 512, 128), WIN)
        flat = nn_dot(att[g, :128], wo[mine, :]) + nn_dot(att_in[g], wo[other, :])
        values = x[:, pl.ds(pl.multiple_of(g * 32, 32), 32), :].astype(jnp.float32)
        u[g] = (values + table[2] * flat.reshape(4, 32, D)).astype(jnp.bfloat16)
        for slot in range(1, 4):
            give(g, slot).start()
        own_give(g).start()

    lax.fori_loop(0, 3, early, 0)
    pass_z(3)
    project(1, 2, 2)
    loads[4].wait()

    def turn(g, carry):
        edge = jnp.zeros((256, 128), jnp.float32)
        edge = late(g, 0, edge)
        edge = late(g, 1, edge)

        @pl.when(g > 0)
        def _():
            finish(g - 1)

        edge = late(g, 2, edge)
        late(g, 3, edge)
        swap(g).start()
        return carry

    lax.fori_loop(0, 3, turn, 0)
    finish(2)

    def spread(g, step):
        return remote(
            grouped.at[g, (frame + step) % 8], t.at[g, frame], g_send.at[g, step], g_recv.at[g, step], peer(step)
        )

    def own_spread(g):
        return pltpu.make_async_copy(grouped.at[g, frame], t.at[g, frame], own_sem.at[1, g])

    def collect(g, step):
        return remote(r.at[g, (frame + step) % 8], back.at[g, frame], r_send.at[g, step], r_recv.at[g, step], peer(step))

    def own_collect(g):
        return pltpu.make_async_copy(r.at[g, frame], back.at[g, frame], own_sem.at[2, g])

    forward = shuffle(True)
    pl.semaphore_wait(meet_sem.at[1], 1)

    def relay(g, carry):
        own_give(g).wait()
        for slot in range(1, 4):
            give(g, slot).wait_recv()
        grouped[g] = nn_dot(forward, gathered[g].reshape(128, D)).astype(jnp.bfloat16).reshape(8, 16, D)
        for step in range(1, 8):
            spread(g, step).start()
        own_spread(g).start()
        return carry

    lax.fori_loop(0, 3, relay, 0)
    loads[5].wait()
    loads[6].wait()

    a = lax.broadcasted_iota(jnp.int32, (128, 128), 0)
    b = lax.broadcasted_iota(jnp.int32, (128, 128), 1)
    bias = jnp.where(a % 4 == b % 4, 0.0, -1e30)
    table1 = [mod[part, 1:2, :] for part in range(3)]

    def block(g, carry):
        own_spread(g).wait()
        for step in range(1, 8):
            spread(g, step).wait_recv()
        values = t[g].reshape(128, D)
        mixed = modulate(values, table1)
        packed[:, :D] = (nn_dot(mixed, wt[:, :D]) * SCALE).astype(jnp.bfloat16)
        packed[:, D : 2 * D] = nn_dot(mixed, wt[:, D : 2 * D]).astype(jnp.bfloat16)
        packed[:, 2 * D :] = nn_dot(mixed, wt[:, 2 * D :]).astype(jnp.bfloat16)
        spots = []
        scores = []
        for h in range(HEADS):
            at = 128 * min(HEAD * h // 128, 7)
            start = HEAD * h - at
            spots.append((at, head_lanes(start), 0 if start else 255))
            queries = choose(packed[:, at : at + 256], spots[h][1])
            scores.append(nt_dot(queries, packed[:, D + at : D + at + 256]) + bias)
        weights = []
        for h in range(HEADS):
            top = jnp.max(scores[h], axis=-1, keepdims=True)
            weights.append(jnp.exp2(scores[h] - top).astype(jnp.bfloat16))
        tiles = [None] * 9
        for h, (at, mine, free) in enumerate(spots):
            part = nn_dot(weights[h], count_in(packed[:, 2 * D + at : 2 * D + at + 256], free))
            part = jnp.where(mine, part * (1.0 / part[:, free : free + 1]), 0.0)
            for side in range(2):
                tile = at // 128 + side
                piece = part[:, 128 * side : 128 * side + 128]
                tiles[tile] = piece if tiles[tile] is None else tiles[tile] + piece
        for tile in range(9):
            mixed_t[:, 128 * tile : 128 * tile + 128] = tiles[tile].astype(jnp.bfloat16)
        flat = nn_dot(mixed_t[...], wto[...])
        r[g] = (values.astype(jnp.float32) + table1[2] * flat).astype(jnp.bfloat16).reshape(8, 16, D)
        for step in range(1, 8):
            collect(g, step).start()
        own_collect(g).start()
        return carry

    lax.fori_loop(0, 3, block, 0)

    backward = shuffle(False)

    def put(g):
        return pltpu.make_async_copy(res.at[g], out.at[:, pl.ds(pl.multiple_of(g * 32, 32), 32), :], o_sem.at[g])

    def settle(g, carry):
        own_collect(g).wait()
        for step in range(1, 8):
            collect(g, step).wait_recv()
        res[g] = nn_dot(backward, back[g].reshape(128, D)).astype(jnp.bfloat16).reshape(4, 32, D)
        put(g).start()
        return carry

    lax.fori_loop(0, 3, settle, 0)

    along_y(2).wait_send()
    along_y(3).wait_send()
    for slot in range(4):
        over_z(slot).wait_send()
        to_sibling(0, slot).wait_send()
        to_sibling(1, slot).wait_send()

    def drain(g, carry):
        swap(g).wait_send()
        for slot in range(1, 4):
            give(g, slot).wait_send()
        for step in range(1, 8):
            spread(g, step).wait_send()
            collect(g, step).wait_send()
        put(g).wait()
        return carry

    lax.fori_loop(0, 3, drain, 0)


def shards(tokens, modulation, spatial_input, spatial_output, temporal_input, temporal_output):
    dma = pltpu.SemaphoreType.DMA
    held = pl.BlockSpec(memory_space=pl.ANY)

    def bf16(*shape):
        return pltpu.VMEM(shape, jnp.bfloat16)

    return pl.pallas_call(
        kernel,
        out_shape=jax.ShapeDtypeStruct((4, 96, D), jnp.bfloat16),
        in_specs=[held, pl.BlockSpec(memory_space=pltpu.VMEM), held, held, held, held],
        out_specs=held,
        scratch_shapes=[
            bf16(4, 96, D),
            bf16(2, 4, 2, 96, D),
            bf16(D, 3 * WIN),
            bf16(D, D),
            bf16(768, WIN),
            bf16(1536, WIN),
            bf16(1536, WIN),
            pltpu.VMEM((8, 768, 256), jnp.float32),
            pltpu.VMEM((8, 768, 128), jnp.float32),
            bf16(3, 256, WIN),
            bf16(3, 128, WIN),
            bf16(3, 4, 32, D),
            bf16(3, 4, 32, D),
            bf16(D, 3 * D),
            bf16(D, D),
            bf16(3, 8, 16, D),
            bf16(3, 8, 16, D),
            bf16(128, 3 * D),
            bf16(128, D),
            bf16(3, 8, 16, D),
            bf16(3, 8, 16, D),
            bf16(3, 4, 32, D),
            dma((7,)),
            dma((4,)), dma((4,)),
            dma((2, 4)), dma((2, 4)),
            dma((4,)), dma((4,)),
            dma((3,)), dma((3,)),
            dma((3, 4)), dma((3, 4)),
            dma((3, 8)), dma((3, 8)),
            dma((3, 8)), dma((3, 8)),
            dma((3, 3)),
            dma((3,)),
            pltpu.SemaphoreType.REGULAR((2,)),
        ],
        compiler_params=pltpu.CompilerParams(
            collective_id=0, has_side_effects=True, vmem_limit_bytes=VMEM_LIMIT
        ),
        name="block_pair",
    )(tokens, jnp.transpose(modulation, (1, 0, 2)), spatial_input, spatial_output, temporal_input, temporal_output)


def solution(mesh):
    in_specs = (P("frame", "patch", None), P(), P(), P(), P(), P())
    out_specs = P("frame", "patch", None)
    return jax.shard_map(shards, mesh=mesh, in_specs=in_specs, out_specs=out_specs, check_vma=False)
```

```python
import math

import jax
import jax.numpy as jnp
from jax import lax
from jax.experimental import pallas as pl
from jax.experimental.pallas import tpu as pltpu
from jax.sharding import PartitionSpec as P

D = 1152
HEADS = 16
HEAD = 72
WIN = 640
EARLY = 768
LATE = 768
PLACES = ((0, 1, 2, 4), (3, 5, 6, 7))
SCALE = math.log2(math.e) / math.sqrt(HEAD)
MESH = pl.DeviceIdType.MESH
VMEM_LIMIT = 60 * 1024 * 1024
STEPS = (0, 1, 3, 2)


def modulate(values, table):
    wide = values.astype(jnp.float32)
    centre = jnp.mean(wide, axis=-1, keepdims=True)
    wide = wide - centre
    spread = jnp.mean(jnp.square(wide), axis=-1, keepdims=True)
    normed = wide * lax.rsqrt(spread + 1e-06)
    return (normed * (1.0 + table[1]) + table[0]).astype(jnp.bfloat16)


def nt_dot(a, b):
    return lax.dot_general(a, b, (((1,), (1,)), ((), ())), preferred_element_type=jnp.float32)


def nn_dot(a, b):
    return jnp.dot(a, b, preferred_element_type=jnp.float32)


def lanes(width):
    return lax.broadcasted_iota(jnp.int32, (1, width), 1)


def head_lanes(start):
    return (lanes(256) >= start) & (lanes(256) < start + HEAD)


def choose(queries, mine):
    return queries * jnp.where(mine, 1.0, 0.0).astype(jnp.bfloat16)


def count_in(values, free):
    one = jnp.where(lanes(256) == free, 1.0, 0.0)
    return values * (1.0 - one).astype(jnp.bfloat16) + one.astype(jnp.bfloat16)


def shuffle(forward):
    a = lax.broadcasted_iota(jnp.int32, (128, 128), 0)
    b = lax.broadcasted_iota(jnp.int32, (128, 128), 1)
    grouped, plain = (a, b) if forward else (b, a)
    source = ((grouped // 4) % 4) * 32 + (grouped // 16) * 4 + grouped % 4
    return jnp.where(source == plain, 1.0, 0.0).astype(jnp.bfloat16)


def kernel(
    tok, mod_in, w_in0, w_out0, w_in1, w_out1, out,
    mod, x, m, w, wo, q, k, v, first, stat, att, att_in, u, gathered,
    wt, wto, grouped, t, packed, mixed_t, r, back, res,
    load_sem, y_send, y_recv, s_send, s_recv, z_send, z_recv, a_send, a_recv,
    u_send, u_recv, g_send, g_recv, r_send, r_recv, own_sem, o_sem, meet_sem,
):
    frame = lax.axis_index("frame")
    patch = lax.axis_index("patch")
    y = patch // 4
    z = (patch // 2) % 2
    core = patch % 2
    sibling = (frame, y * 4 + z * 2 + (1 - core))
    across = (frame, y * 4 + (1 - z) * 2 + core)

    def along(step):
        return (frame, ((y + step) % 4) * 4 + z * 2 + core)

    def peer(step):
        return ((frame + step) % 8, patch)

    def beside_x(step):
        return ((frame // 4) * 4 + (frame + step) % 4, patch)

    opposite = ((frame + 4) % 8, patch)
    over_edge = ((frame + 4) % 8, y * 4 + (1 - z) * 2 + core)

    loads = [pltpu.make_async_copy(tok.at[y], x.at[0], load_sem.at[0])]
    for part in range(3):
        columns = pl.ds(pl.multiple_of(part * D + core * 512, 128), WIN)
        loads.append(
            pltpu.make_async_copy(w_in0.at[:, columns], w.at[:, pl.ds(part * WIN, WIN)], load_sem.at[1 + part])
        )
    loads.append(pltpu.make_async_copy(w_out0, wo, load_sem.at[4]))
    loads.append(pltpu.make_async_copy(w_in1, wt, load_sem.at[5]))
    loads.append(pltpu.make_async_copy(w_out1, wto, load_sem.at[6]))
    loads.append(pltpu.make_async_copy(mod_in, mod, load_sem.at[7]))
    for load in [loads[7]] + loads[:4]:
        load.start()

    barrier = pltpu.get_barrier_semaphore()
    beside = [beside_x(1), beside_x(3)]
    greeted = [sibling, across] + [along(s) for s in (1, 2, 3)] + beside + [over_edge]
    for device in greeted:
        pl.semaphore_signal(barrier, inc=1, device_id=device, device_id_type=MESH)
    loads[7].wait()
    table = [mod[part, 0:1, :] for part in range(3)]
    loads[0].wait()
    m[0, 0, 0] = modulate(x[0], table)
    pl.semaphore_wait(barrier, len(greeted))

    for device in beside + [across]:
        pl.semaphore_signal(meet_sem.at[0], inc=1, device_id=device, device_id_type=MESH)

    def remote(src, dst, send, recv, device):
        return pltpu.make_async_remote_copy(
            src_ref=src, dst_ref=dst, send_sem=send, recv_sem=recv, device_id=device, device_id_type=MESH
        )

    def rows_of(piece):
        return pl.ds(piece * 48, 48)

    def along_y(slot, piece):
        step = STEPS[slot]
        rows = rows_of(piece)
        return remote(
            tok.at[(y + 4 - step) % 4, rows], x.at[slot, rows],
            y_send.at[slot, piece], y_recv.at[slot, piece], along(4 - step),
        )

    def over_z(slot, piece):
        rows = rows_of(piece)
        return remote(
            m.at[0, slot, 0, rows], m.at[1, slot, 0, rows], z_send.at[slot, piece], z_recv.at[slot, piece], across
        )

    def to_sibling(half, slot, piece):
        rows = rows_of(piece)
        return remote(
            m.at[half, slot, 0, rows], m.at[half, slot, 1, rows],
            s_send.at[half, slot, piece], s_recv.at[half, slot, piece], sibling,
        )

    def arrive(slot, piece):
        along_y(slot, piece).wait_recv()
        rows = rows_of(piece)
        m[0, slot, 0, rows] = modulate(x[slot, rows], table)
        over_z(slot, piece).start()
        to_sibling(0, slot, piece).start()

    def pass_z(slot):
        for piece in range(2):
            over_z(slot, piece).wait_recv()
            to_sibling(1, slot, piece).start()

    def project(half, slot, count, quarters=(0, 1)):
        if 1 in quarters:
            for n in range(count):
                for piece in range(2):
                    to_sibling(half, slot + n, piece).wait_recv()
        chosen = slice(quarters[0], quarters[-1] + 1)
        mixed = m[half, slot : slot + count, chosen].reshape(96 * len(quarters) * count, D)
        flat = nn_dot(mixed, w[...] if half == 0 else w[:, WIN:])
        if half == 0:
            queries = (flat[:, :WIN] * SCALE).astype(jnp.bfloat16)
            flat = flat[:, WIN:]
        flat = flat.astype(jnp.bfloat16)
        for n in range(count):
            for index, quarter in enumerate(quarters):
                at = (n * len(quarters) + index) * 96
                if half == 0:
                    q[quarter, slot + n] = queries[at : at + 96].reshape(3, 32, WIN)
                rows = pl.ds(PLACES[half][slot + n] * 192 + quarter * 96, 96)
                k[rows, :] = flat[at : at + 96, :WIN]
                v[rows, :] = flat[at : at + 96, WIN:]

    for piece in range(2):
        along_y(1, piece).start()
        along_y(2, piece).start()
    for piece in range(2):
        over_z(0, piece).start()
        to_sibling(0, 0, piece).start()
    for load in loads[1:4]:
        load.wait()
    for load in loads[4:7]:
        load.start()
    project(0, 0, 1)
    arrive(1, 0)
    arrive(2, 0)
    for piece in range(2):
        along_y(1, piece).wait_send()
        along_y(3, piece).start()
    arrive(1, 1)
    arrive(2, 1)
    project(0, 1, 2, (0,))
    pass_z(0)
    project(0, 1, 2, (1,))
    project(1, 0, 1)
    pl.semaphore_wait(meet_sem.at[0], 3)
    pl.semaphore_signal(meet_sem.at[1], inc=1, device_id=opposite, device_id_type=MESH)

    def starts(j):
        return ((16 * j + 64 * core, 255), (16 * j + 72 + 64 * core, 0))

    def early(part, count):
        for j in range(4):
            window = slice(128 * j, 128 * j + 256)
            queries = q[part + (slice(None), slice(None), window)]
            shape = queries.shape[:3]
            queries, keys, values = queries.reshape(count, 256), k[:EARLY, window], v[:EARLY, window]
            for odd, (start, free) in enumerate(starts(j)):
                scores = nt_dot(choose(queries, head_lanes(start)), keys)
                top = jnp.max(scores, axis=-1, keepdims=True)
                weights = jnp.exp2(scores - top).astype(jnp.bfloat16)
                total = nn_dot(weights, count_in(values, free))
                first[(2 * j + odd,) + part] = total.reshape(shape + (256,))
                stat[(2 * j + odd,) + part] = jnp.broadcast_to(top, (count, 128)).reshape(shape + (128,))

    def late(g, j, carry):
        window = slice(128 * j, 128 * j + 256)
        queries = q[:, :, g, :, window].reshape(256, 256)
        keys, values = k[EARLY:, window], v[EARLY:, window]
        both = jnp.zeros((256, 256), jnp.float32)
        for odd, (start, free) in enumerate(starts(j)):
            h = 2 * j + odd
            mine = head_lanes(start)
            scores = nt_dot(choose(queries, mine), keys)
            parts = [scores[:, 128 * n : 128 * n + 128] for n in range(LATE // 128)]
            top = parts[0]
            for piece in parts[1:]:
                top = jnp.maximum(top, piece)
            before = stat[h, :, :, g].reshape(256, 128)
            top = jnp.maximum(before, jnp.max(top, axis=-1, keepdims=True))
            weights = jnp.concatenate([jnp.exp2(piece - top).astype(jnp.bfloat16) for piece in parts], axis=1)
            part = nn_dot(weights, count_in(values, free))
            shrink = jnp.exp2(before - top)
            earlier = first[h, :, :, g].reshape(256, 256)
            total = jnp.concatenate(
                [part[:, :128] + earlier[:, :128] * shrink, part[:, 128:] + earlier[:, 128:] * shrink], axis=1
            )
            both = jnp.where(mine, total * (1.0 / total[:, free : free + 1]), both)
        att[g, :, 128 * j : 128 * j + 128] = (carry + both[:, :128]).astype(jnp.bfloat16)
        if j == 3:
            att[g, :, 512:] = both[:, 128:].astype(jnp.bfloat16)
        return both[:, 128:]

    def swap(g):
        return remote(att.at[g, pl.ds(128, 128)], att_in.at[g], a_send.at[g], a_recv.at[g], sibling)

    def give(g, slot):
        return remote(u.at[g, slot], gathered.at[g, y], u_send.at[g, slot], u_recv.at[g, slot], along(STEPS[slot]))

    def own_give(g):
        return pltpu.make_async_copy(u.at[g, 0], gathered.at[g, y], own_sem.at[0, g])

    def finish(g):
        swap(g).wait_recv()
        mine = pl.ds(pl.multiple_of(core * 512, 128), WIN)
        other = pl.ds(pl.multiple_of((1 - core) * 512, 128), WIN)
        flat = nn_dot(att[g, :128], wo[mine, :]) + nn_dot(att_in[g], wo[other, :])
        values = x[:, pl.ds(pl.multiple_of(g * 32, 32), 32), :].astype(jnp.float32)
        u[g] = (values + table[2] * flat.reshape(4, 32, D)).astype(jnp.bfloat16)
        for slot in range(1, 4):
            give(g, slot).start()
        own_give(g).start()

    early((0, slice(0, 3)), 288)
    arrive(3, 0)
    arrive(3, 1)
    early((1, slice(0, 3)), 288)
    project(0, 3, 1)
    pass_z(1)
    pass_z(2)
    early((slice(0, 2), 3), 192)
    project(1, 1, 2)
    pass_z(3)
    project(1, 3, 1)
    loads[4].wait()

    def turn(g, carry):
        edge = jnp.zeros((256, 128), jnp.float32)
        edge = late(g, 0, edge)
        edge = late(g, 1, edge)

        @pl.when(g > 0)
        def _():
            finish(g - 1)

        edge = late(g, 2, edge)
        late(g, 3, edge)
        swap(g).start()
        return carry

    lax.fori_loop(0, 3, turn, 0)
    finish(2)

    def spread(g, step):
        return remote(
            grouped.at[g, (frame + step) % 8], t.at[g, frame], g_send.at[g, step], g_recv.at[g, step], peer(step)
        )

    def own_spread(g):
        return pltpu.make_async_copy(grouped.at[g, frame], t.at[g, frame], own_sem.at[1, g])

    def collect(g, step):
        return remote(r.at[g, (frame + step) % 8], back.at[g, frame], r_send.at[g, step], r_recv.at[g, step], peer(step))

    def own_collect(g):
        return pltpu.make_async_copy(r.at[g, frame], back.at[g, frame], own_sem.at[2, g])

    forward = shuffle(True)
    pl.semaphore_wait(meet_sem.at[1], 1)

    def relay(g, carry):
        own_give(g).wait()
        for slot in range(1, 4):
            give(g, slot).wait_recv()
        grouped[g] = nn_dot(forward, gathered[g].reshape(128, D)).astype(jnp.bfloat16).reshape(8, 16, D)
        for step in range(1, 8):
            spread(g, step).start()
        own_spread(g).start()
        return carry

    lax.fori_loop(0, 3, relay, 0)
    loads[5].wait()
    loads[6].wait()

    a = lax.broadcasted_iota(jnp.int32, (128, 128), 0)
    b = lax.broadcasted_iota(jnp.int32, (128, 128), 1)
    bias = jnp.where(a % 4 == b % 4, 0.0, -1e30)
    table1 = [mod[part, 1:2, :] for part in range(3)]

    def block(g, carry):
        own_spread(g).wait()
        for step in range(1, 8):
            spread(g, step).wait_recv()
        values = t[g].reshape(128, D)
        mixed = modulate(values, table1)
        packed[:, :D] = (nn_dot(mixed, wt[:, :D]) * SCALE).astype(jnp.bfloat16)
        packed[:, D : 2 * D] = nn_dot(mixed, wt[:, D : 2 * D]).astype(jnp.bfloat16)
        packed[:, 2 * D :] = nn_dot(mixed, wt[:, 2 * D :]).astype(jnp.bfloat16)
        spots = []
        scores = []
        for h in range(HEADS):
            at = 128 * min(HEAD * h // 128, 7)
            start = HEAD * h - at
            spots.append((at, head_lanes(start), 0 if start else 255))
            queries = choose(packed[:, at : at + 256], spots[h][1])
            scores.append(nt_dot(queries, packed[:, D + at : D + at + 256]) + bias)
        weights = []
        for h in range(HEADS):
            top = jnp.max(scores[h], axis=-1, keepdims=True)
            weights.append(jnp.exp2(scores[h] - top).astype(jnp.bfloat16))
        tiles = [None] * 9
        for h, (at, mine, free) in enumerate(spots):
            part = nn_dot(weights[h], count_in(packed[:, 2 * D + at : 2 * D + at + 256], free))
            part = jnp.where(mine, part * (1.0 / part[:, free : free + 1]), 0.0)
            for side in range(2):
                tile = at // 128 + side
                piece = part[:, 128 * side : 128 * side + 128]
                tiles[tile] = piece if tiles[tile] is None else tiles[tile] + piece
        for tile in range(9):
            mixed_t[:, 128 * tile : 128 * tile + 128] = tiles[tile].astype(jnp.bfloat16)
        flat = nn_dot(mixed_t[...], wto[...])
        r[g] = (values.astype(jnp.float32) + table1[2] * flat).astype(jnp.bfloat16).reshape(8, 16, D)
        for step in range(1, 8):
            collect(g, step).start()
        own_collect(g).start()
        return carry

    lax.fori_loop(0, 3, block, 0)

    backward = shuffle(False)

    def put(g):
        return pltpu.make_async_copy(res.at[g], out.at[:, pl.ds(pl.multiple_of(g * 32, 32), 32), :], o_sem.at[g])

    def settle(g, carry):
        own_collect(g).wait()
        for step in range(1, 8):
            collect(g, step).wait_recv()
        res[g] = nn_dot(backward, back[g].reshape(128, D)).astype(jnp.bfloat16).reshape(4, 32, D)
        put(g).start()
        return carry

    lax.fori_loop(0, 3, settle, 0)

    for piece in range(2):
        along_y(2, piece).wait_send()
        along_y(3, piece).wait_send()
        for slot in range(4):
            over_z(slot, piece).wait_send()
            to_sibling(0, slot, piece).wait_send()
            to_sibling(1, slot, piece).wait_send()

    def drain(g, carry):
        swap(g).wait_send()
        for slot in range(1, 4):
            give(g, slot).wait_send()
        for step in range(1, 8):
            spread(g, step).wait_send()
            collect(g, step).wait_send()
        put(g).wait()
        return carry

    lax.fori_loop(0, 3, drain, 0)


def shards(tokens, modulation, spatial_input, spatial_output, temporal_input, temporal_output):
    dma = pltpu.SemaphoreType.DMA
    held = pl.BlockSpec(memory_space=pl.ANY)

    def bf16(*shape):
        return pltpu.VMEM(shape, jnp.bfloat16)

    return pl.pallas_call(
        kernel,
        out_shape=jax.ShapeDtypeStruct((4, 96, D), jnp.bfloat16),
        in_specs=[held] * 6,
        out_specs=held,
        scratch_shapes=[
            pltpu.VMEM((3, 2, D), jnp.float32),
            bf16(4, 96, D),
            bf16(2, 4, 2, 96, D),
            bf16(D, 3 * WIN),
            bf16(D, D),
            bf16(2, 4, 3, 32, WIN),
            bf16(1536, WIN),
            bf16(1536, WIN),
            pltpu.VMEM((8, 2, 4, 3, 32, 256), jnp.float32),
            pltpu.VMEM((8, 2, 4, 3, 32, 128), jnp.float32),
            bf16(3, 256, WIN),
            bf16(3, 128, WIN),
            bf16(3, 4, 32, D),
            bf16(3, 4, 32, D),
            bf16(D, 3 * D),
            bf16(D, D),
            bf16(3, 8, 16, D),
            bf16(3, 8, 16, D),
            bf16(128, 3 * D),
            bf16(128, D),
            bf16(3, 8, 16, D),
            bf16(3, 8, 16, D),
            bf16(3, 4, 32, D),
            dma((8,)),
            dma((4, 2)), dma((4, 2)),
            dma((2, 4, 2)), dma((2, 4, 2)),
            dma((4, 2)), dma((4, 2)),
            dma((3,)), dma((3,)),
            dma((3, 4)), dma((3, 4)),
            dma((3, 8)), dma((3, 8)),
            dma((3, 8)), dma((3, 8)),
            dma((3, 3)),
            dma((3,)),
            pltpu.SemaphoreType.REGULAR((2,)),
        ],
        compiler_params=pltpu.CompilerParams(
            collective_id=0, has_side_effects=True, vmem_limit_bytes=VMEM_LIMIT
        ),
        name="block_pair",
    )(tokens, jnp.transpose(modulation, (1, 0, 2)), spatial_input, spatial_output, temporal_input, temporal_output)


def solution(mesh):
    in_specs = (P("frame", "patch", None), P(), P(), P(), P(), P())
    out_specs = P("frame", "patch", None)
    return jax.shard_map(shards, mesh=mesh, in_specs=in_specs, out_specs=out_specs, check_vma=False)
```

```python
import math

import jax
import jax.numpy as jnp
from jax import lax
from jax.experimental import pallas as pl
from jax.experimental.pallas import tpu as pltpu
from jax.sharding import PartitionSpec as P

D = 1152
HEADS = 16
HEAD = 72
WIN = 640
EARLY = 768
LATE = 768
PLACES = ((0, 1, 2, 4), (3, 5, 6, 7))
SCALE = math.log2(math.e) / math.sqrt(HEAD)
MESH = pl.DeviceIdType.MESH
VMEM_LIMIT = 60 * 1024 * 1024
STEPS = (0, 1, 3, 2)


def modulate(values, table):
    wide = values.astype(jnp.float32)
    centre = jnp.mean(wide, axis=-1, keepdims=True)
    wide = wide - centre
    spread = jnp.mean(jnp.square(wide), axis=-1, keepdims=True)
    normed = wide * lax.rsqrt(spread + 1e-06)
    return (normed * (1.0 + table[1]) + table[0]).astype(jnp.bfloat16)


def nt_dot(a, b):
    return lax.dot_general(a, b, (((1,), (1,)), ((), ())), preferred_element_type=jnp.float32)


def nn_dot(a, b):
    return jnp.dot(a, b, preferred_element_type=jnp.float32)


def lanes(width):
    return lax.broadcasted_iota(jnp.int32, (1, width), 1)


def head_lanes(start):
    return (lanes(256) >= start) & (lanes(256) < start + HEAD)


def choose(queries, mine):
    return queries * jnp.where(mine, 1.0, 0.0).astype(jnp.bfloat16)


def count_in(values, free):
    one = jnp.where(lanes(256) == free, 1.0, 0.0)
    return values * (1.0 - one).astype(jnp.bfloat16) + one.astype(jnp.bfloat16)


def shuffle(forward):
    a = lax.broadcasted_iota(jnp.int32, (128, 128), 0)
    b = lax.broadcasted_iota(jnp.int32, (128, 128), 1)
    grouped, plain = (a, b) if forward else (b, a)
    source = ((grouped // 4) % 4) * 32 + (grouped // 16) * 4 + grouped % 4
    return jnp.where(source == plain, 1.0, 0.0).astype(jnp.bfloat16)


def kernel(
    tok, mod_in, w_in0, w_out0, w_in1, w_out1, out,
    mod, x, m, w, wo, q, k, v, first, stat, att, att_in, u, gathered,
    wt, wto, grouped, t, packed, mixed_t, r, back, res,
    load_sem, y_send, y_recv, s_send, s_recv, z_send, z_recv, a_send, a_recv,
    u_send, u_recv, g_send, g_recv, r_send, r_recv, own_sem, o_sem, meet_sem,
):
    frame = lax.axis_index("frame")
    patch = lax.axis_index("patch")
    y = patch // 4
    z = (patch // 2) % 2
    core = patch % 2
    sibling = (frame, y * 4 + z * 2 + (1 - core))
    across = (frame, y * 4 + (1 - z) * 2 + core)

    def along(step):
        return (frame, ((y + step) % 4) * 4 + z * 2 + core)

    def peer(step):
        return ((frame + step) % 8, patch)

    def beside_x(step):
        return ((frame // 4) * 4 + (frame + step) % 4, patch)

    opposite = ((frame + 4) % 8, patch)
    over_edge = ((frame + 4) % 8, y * 4 + (1 - z) * 2 + core)

    loads = [pltpu.make_async_copy(tok.at[y], x.at[0], load_sem.at[0])]
    for part in range(3):
        columns = pl.ds(pl.multiple_of(part * D + core * 512, 128), WIN)
        loads.append(
            pltpu.make_async_copy(w_in0.at[:, columns], w.at[:, pl.ds(part * WIN, WIN)], load_sem.at[1 + part])
        )
    loads.append(pltpu.make_async_copy(w_out0, wo, load_sem.at[4]))
    loads.append(pltpu.make_async_copy(w_in1, wt, load_sem.at[5]))
    loads.append(pltpu.make_async_copy(w_out1, wto, load_sem.at[6]))
    loads.append(pltpu.make_async_copy(mod_in, mod, load_sem.at[7]))
    for load in [loads[7]] + loads[:4]:
        load.start()

    barrier = pltpu.get_barrier_semaphore()
    beside = [beside_x(1), beside_x(3)]
    greeted = [sibling, across] + [along(s) for s in (1, 2, 3)] + beside + [over_edge]
    for device in greeted:
        pl.semaphore_signal(barrier, inc=1, device_id=device, device_id_type=MESH)
    loads[7].wait()
    table = [mod[part, 0:1, :] for part in range(3)]
    loads[0].wait()
    m[0, 0, 0] = modulate(x[0], table)
    pl.semaphore_wait(barrier, len(greeted))

    for device in beside + [across]:
        pl.semaphore_signal(meet_sem.at[0], inc=1, device_id=device, device_id_type=MESH)

    def remote(src, dst, send, recv, device):
        return pltpu.make_async_remote_copy(
            src_ref=src, dst_ref=dst, send_sem=send, recv_sem=recv, device_id=device, device_id_type=MESH
        )

    def rows_of(piece):
        return pl.ds(piece * 48, 48)

    def along_y(slot, piece):
        step = STEPS[slot]
        rows = rows_of(piece)
        return remote(
            tok.at[(y + 4 - step) % 4, rows], x.at[slot, rows],
            y_send.at[slot, piece], y_recv.at[slot, piece], along(4 - step),
        )

    def over_z(slot, piece):
        rows = rows_of(piece)
        return remote(
            m.at[0, slot, 0, rows], m.at[1, slot, 0, rows], z_send.at[slot, piece], z_recv.at[slot, piece], across
        )

    def to_sibling(half, slot, piece):
        rows = rows_of(piece)
        return remote(
            m.at[half, slot, 0, rows], m.at[half, slot, 1, rows],
            s_send.at[half, slot, piece], s_recv.at[half, slot, piece], sibling,
        )

    def arrive(slot, piece):
        along_y(slot, piece).wait_recv()
        rows = rows_of(piece)
        m[0, slot, 0, rows] = modulate(x[slot, rows], table)
        over_z(slot, piece).start()
        to_sibling(0, slot, piece).start()

    def pass_z(slot):
        for piece in range(2):
            over_z(slot, piece).wait_recv()
            to_sibling(1, slot, piece).start()

    def project(half, slot, count, quarters=(0, 1)):
        if 1 in quarters:
            for n in range(count):
                for piece in range(2):
                    to_sibling(half, slot + n, piece).wait_recv()
        chosen = slice(quarters[0], quarters[-1] + 1)
        mixed = m[half, slot : slot + count, chosen].reshape(96 * len(quarters) * count, D)
        flat = nn_dot(mixed, w[...] if half == 0 else w[:, WIN:])
        if half == 0:
            queries = (flat[:, :WIN] * SCALE).astype(jnp.bfloat16)
            flat = flat[:, WIN:]
        flat = flat.astype(jnp.bfloat16)
        for n in range(count):
            for index, quarter in enumerate(quarters):
                at = (n * len(quarters) + index) * 96
                if half == 0:
                    q[quarter, slot + n] = queries[at : at + 96].reshape(3, 32, WIN)
                rows = pl.ds(PLACES[half][slot + n] * 192 + quarter * 96, 96)
                k[rows, :] = flat[at : at + 96, :WIN]
                v[rows, :] = flat[at : at + 96, WIN:]

    for piece in range(2):
        along_y(1, piece).start()
        along_y(2, piece).start()
    for piece in range(2):
        over_z(0, piece).start()
        to_sibling(0, 0, piece).start()
    for load in loads[1:4]:
        load.wait()
    for load in loads[4:7]:
        load.start()
    project(0, 0, 1)
    arrive(1, 0)
    arrive(2, 0)
    for piece in range(2):
        along_y(1, piece).wait_send()
        along_y(3, piece).start()
    arrive(1, 1)
    arrive(2, 1)
    project(0, 1, 2, (0,))
    pass_z(0)
    project(0, 1, 2, (1,))
    project(1, 0, 1)
    pl.semaphore_wait(meet_sem.at[0], 3)
    pl.semaphore_signal(meet_sem.at[1], inc=1, device_id=opposite, device_id_type=MESH)

    def starts(j):
        return ((16 * j + 64 * core, 255), (16 * j + 72 + 64 * core, 0))

    def early(parts):
        for j in range(4):
            window = slice(128 * j, 128 * j + 256)
            pieces = [q[part + (Ellipsis, window)] for part in parts]
            shapes = [piece.shape[:-1] for piece in pieces]
            counts = [math.prod(shape) for shape in shapes]
            pieces = [piece.reshape(count, 256) for piece, count in zip(pieces, counts)]
            queries = pieces[0] if len(pieces) == 1 else jnp.concatenate(pieces, axis=0)
            keys, values = k[:EARLY, window], v[:EARLY, window]
            for odd, (start, free) in enumerate(starts(j)):
                scores = nt_dot(choose(queries, head_lanes(start)), keys)
                top = jnp.max(scores, axis=-1, keepdims=True)
                weights = jnp.exp2(scores - top).astype(jnp.bfloat16)
                total = nn_dot(weights, count_in(values, free))
                top = jnp.broadcast_to(top, (sum(counts), 128))
                at = 0
                for part, shape, count in zip(parts, shapes, counts):
                    first[(2 * j + odd,) + part] = total[at : at + count].reshape(shape + (256,))
                    stat[(2 * j + odd,) + part] = top[at : at + count].reshape(shape + (128,))
                    at += count

    def early_rest(g):
        early([(1, slice(0, 3), g), (slice(0, 2), 3, g)])

    def late(g, j, carry):
        window = slice(128 * j, 128 * j + 256)
        queries = q[:, :, g, :, window].reshape(256, 256)
        keys, values = k[EARLY:, window], v[EARLY:, window]
        both = jnp.zeros((256, 256), jnp.float32)
        for odd, (start, free) in enumerate(starts(j)):
            h = 2 * j + odd
            mine = head_lanes(start)
            scores = nt_dot(choose(queries, mine), keys)
            parts = [scores[:, 128 * n : 128 * n + 128] for n in range(LATE // 128)]
            top = parts[0]
            for piece in parts[1:]:
                top = jnp.maximum(top, piece)
            before = stat[h, :, :, g].reshape(256, 128)
            top = jnp.maximum(before, jnp.max(top, axis=-1, keepdims=True))
            weights = jnp.concatenate([jnp.exp2(piece - top).astype(jnp.bfloat16) for piece in parts], axis=1)
            part = nn_dot(weights, count_in(values, free))
            shrink = jnp.exp2(before - top)
            earlier = first[h, :, :, g].reshape(256, 256)
            total = jnp.concatenate(
                [part[:, :128] + earlier[:, :128] * shrink, part[:, 128:] + earlier[:, 128:] * shrink], axis=1
            )
            both = jnp.where(mine, total * (1.0 / total[:, free : free + 1]), both)
        att[g, :, 128 * j : 128 * j + 128] = (carry + both[:, :128]).astype(jnp.bfloat16)
        if j == 3:
            att[g, :, 512:] = both[:, 128:].astype(jnp.bfloat16)
        return both[:, 128:]

    def swap(g):
        return remote(att.at[g, pl.ds(128, 128)], att_in.at[g], a_send.at[g], a_recv.at[g], sibling)

    def give(g, slot):
        return remote(u.at[g, slot], gathered.at[g, y], u_send.at[g, slot], u_recv.at[g, slot], along(STEPS[slot]))

    def own_give(g):
        return pltpu.make_async_copy(u.at[g, 0], gathered.at[g, y], own_sem.at[0, g])

    def finish(g):
        swap(g).wait_recv()
        mine = pl.ds(pl.multiple_of(core * 512, 128), WIN)
        other = pl.ds(pl.multiple_of((1 - core) * 512, 128), WIN)
        flat = nn_dot(att[g, :128], wo[mine, :]) + nn_dot(att_in[g], wo[other, :])
        values = x[:, pl.ds(pl.multiple_of(g * 32, 32), 32), :].astype(jnp.float32)
        u[g] = (values + table[2] * flat.reshape(4, 32, D)).astype(jnp.bfloat16)
        for slot in range(1, 4):
            give(g, slot).start()
        own_give(g).start()

    def spread(g, step):
        return remote(
            grouped.at[g, (frame + step) % 8], t.at[g, frame], g_send.at[g, step], g_recv.at[g, step], peer(step)
        )

    def own_spread(g):
        return pltpu.make_async_copy(grouped.at[g, frame], t.at[g, frame], own_sem.at[1, g])

    def collect(g, step):
        return remote(r.at[g, (frame + step) % 8], back.at[g, frame], r_send.at[g, step], r_recv.at[g, step], peer(step))

    def own_collect(g):
        return pltpu.make_async_copy(r.at[g, frame], back.at[g, frame], own_sem.at[2, g])

    def relay(g):
        own_give(g).wait()
        for slot in range(1, 4):
            give(g, slot).wait_recv()
        grouped[g] = nn_dot(forward, gathered[g].reshape(128, D)).astype(jnp.bfloat16).reshape(8, 16, D)
        for step in range(1, 8):
            spread(g, step).start()
        own_spread(g).start()

    early([(0, slice(0, 3))])
    arrive(3, 0)
    arrive(3, 1)
    project(0, 3, 1)
    early_rest(0)
    pass_z(1)
    pass_z(2)
    early_rest(1)
    project(1, 1, 2)
    pass_z(3)
    project(1, 3, 1)
    loads[4].wait()

    edge = jnp.zeros((256, 128), jnp.float32)

    def late_pairs(g, pairs, edge):
        for j in pairs:
            edge = late(g, j, edge)
        return edge

    late_pairs(0, range(4), edge)
    swap(0).start()
    early_rest(2)
    finish(0)
    late_pairs(1, range(4), edge)
    swap(1).start()
    half = late_pairs(2, range(2), edge)
    finish(1)
    late_pairs(2, range(2, 4), half)
    swap(2).start()
    pl.semaphore_wait(meet_sem.at[1], 1)
    forward = shuffle(True)
    relay(0)
    finish(2)
    relay(1)
    relay(2)

    loads[5].wait()
    loads[6].wait()

    a = lax.broadcasted_iota(jnp.int32, (128, 128), 0)
    b = lax.broadcasted_iota(jnp.int32, (128, 128), 1)
    bias = jnp.where(a % 4 == b % 4, 0.0, -1e30)
    table1 = [mod[part, 1:2, :] for part in range(3)]

    def block(g, carry):
        own_spread(g).wait()
        for step in range(1, 8):
            spread(g, step).wait_recv()
        values = t[g].reshape(128, D)
        mixed = modulate(values, table1)
        packed[:, :D] = (nn_dot(mixed, wt[:, :D]) * SCALE).astype(jnp.bfloat16)
        packed[:, D : 2 * D] = nn_dot(mixed, wt[:, D : 2 * D]).astype(jnp.bfloat16)
        packed[:, 2 * D :] = nn_dot(mixed, wt[:, 2 * D :]).astype(jnp.bfloat16)
        spots = []
        scores = []
        for h in range(HEADS):
            at = 128 * min(HEAD * h // 128, 7)
            start = HEAD * h - at
            spots.append((at, head_lanes(start), 0 if start else 255))
            queries = choose(packed[:, at : at + 256], spots[h][1])
            scores.append(nt_dot(queries, packed[:, D + at : D + at + 256]) + bias)
        weights = []
        for h in range(HEADS):
            top = jnp.max(scores[h], axis=-1, keepdims=True)
            weights.append(jnp.exp2(scores[h] - top).astype(jnp.bfloat16))
        tiles = [None] * 9
        for h, (at, mine, free) in enumerate(spots):
            part = nn_dot(weights[h], count_in(packed[:, 2 * D + at : 2 * D + at + 256], free))
            part = jnp.where(mine, part * (1.0 / part[:, free : free + 1]), 0.0)
            for side in range(2):
                tile = at // 128 + side
                piece = part[:, 128 * side : 128 * side + 128]
                tiles[tile] = piece if tiles[tile] is None else tiles[tile] + piece
        for tile in range(9):
            mixed_t[:, 128 * tile : 128 * tile + 128] = tiles[tile].astype(jnp.bfloat16)
        flat = nn_dot(mixed_t[...], wto[...])
        r[g] = (values.astype(jnp.float32) + table1[2] * flat).astype(jnp.bfloat16).reshape(8, 16, D)
        for step in range(1, 8):
            collect(g, step).start()
        own_collect(g).start()
        return carry

    lax.fori_loop(0, 3, block, 0)

    backward = shuffle(False)

    def put(g):
        return pltpu.make_async_copy(res.at[g], out.at[:, pl.ds(pl.multiple_of(g * 32, 32), 32), :], o_sem.at[g])

    def settle(g, carry):
        own_collect(g).wait()
        for step in range(1, 8):
            collect(g, step).wait_recv()
        res[g] = nn_dot(backward, back[g].reshape(128, D)).astype(jnp.bfloat16).reshape(4, 32, D)
        put(g).start()
        return carry

    lax.fori_loop(0, 3, settle, 0)

    for piece in range(2):
        along_y(2, piece).wait_send()
        along_y(3, piece).wait_send()
        for slot in range(4):
            over_z(slot, piece).wait_send()
            to_sibling(0, slot, piece).wait_send()
            to_sibling(1, slot, piece).wait_send()

    def drain(g, carry):
        swap(g).wait_send()
        for slot in range(1, 4):
            give(g, slot).wait_send()
        for step in range(1, 8):
            spread(g, step).wait_send()
            collect(g, step).wait_send()
        put(g).wait()
        return carry

    lax.fori_loop(0, 3, drain, 0)


def shards(tokens, modulation, spatial_input, spatial_output, temporal_input, temporal_output):
    dma = pltpu.SemaphoreType.DMA
    held = pl.BlockSpec(memory_space=pl.ANY)

    def bf16(*shape):
        return pltpu.VMEM(shape, jnp.bfloat16)

    return pl.pallas_call(
        kernel,
        out_shape=jax.ShapeDtypeStruct((4, 96, D), jnp.bfloat16),
        in_specs=[held] * 6,
        out_specs=held,
        scratch_shapes=[
            pltpu.VMEM((3, 2, D), jnp.float32),
            bf16(4, 96, D),
            bf16(2, 4, 2, 96, D),
            bf16(D, 3 * WIN),
            bf16(D, D),
            bf16(2, 4, 3, 32, WIN),
            bf16(1536, WIN),
            bf16(1536, WIN),
            pltpu.VMEM((8, 2, 4, 3, 32, 256), jnp.float32),
            pltpu.VMEM((8, 2, 4, 3, 32, 128), jnp.float32),
            bf16(3, 256, WIN),
            bf16(3, 128, WIN),
            bf16(3, 4, 32, D),
            bf16(3, 4, 32, D),
            bf16(D, 3 * D),
            bf16(D, D),
            bf16(3, 8, 16, D),
            bf16(3, 8, 16, D),
            bf16(128, 3 * D),
            bf16(128, D),
            bf16(3, 8, 16, D),
            bf16(3, 8, 16, D),
            bf16(3, 4, 32, D),
            dma((8,)),
            dma((4, 2)), dma((4, 2)),
            dma((2, 4, 2)), dma((2, 4, 2)),
            dma((4, 2)), dma((4, 2)),
            dma((3,)), dma((3,)),
            dma((3, 4)), dma((3, 4)),
            dma((3, 8)), dma((3, 8)),
            dma((3, 8)), dma((3, 8)),
            dma((3, 3)),
            dma((3,)),
            pltpu.SemaphoreType.REGULAR((2,)),
        ],
        compiler_params=pltpu.CompilerParams(
            collective_id=0, has_side_effects=True, vmem_limit_bytes=VMEM_LIMIT
        ),
        name="block_pair",
    )(tokens, jnp.transpose(modulation, (1, 0, 2)), spatial_input, spatial_output, temporal_input, temporal_output)


def solution(mesh):
    in_specs = (P("frame", "patch", None), P(), P(), P(), P(), P())
    out_specs = P("frame", "patch", None)
    return jax.shard_map(shards, mesh=mesh, in_specs=in_specs, out_specs=out_specs, check_vma=False)
```

```python
import math

import jax
import jax.numpy as jnp
from jax import lax
from jax.experimental import pallas as pl
from jax.experimental.pallas import tpu as pltpu
from jax.sharding import PartitionSpec as P

D = 1152
HEADS = 16
HEAD = 72
WIN = 640
EARLY = 768
LATE = 768
PLACES = ((0, 1, 2, 4), (3, 5, 6, 7))
SCALE = math.log2(math.e) / math.sqrt(HEAD)
MESH = pl.DeviceIdType.MESH
VMEM_LIMIT = 60 * 1024 * 1024
FAR_FIRST = (6, 5, 2, 7, 1, 4, 3)
STEPS = (0, 1, 3, 2)


def modulate(values, table):
    wide = values.astype(jnp.float32)
    centre = jnp.mean(wide, axis=-1, keepdims=True)
    wide = wide - centre
    spread = jnp.mean(jnp.square(wide), axis=-1, keepdims=True)
    normed = wide * lax.rsqrt(spread + 1e-06)
    return (normed * (1.0 + table[1]) + table[0]).astype(jnp.bfloat16)


def nt_dot(a, b):
    return lax.dot_general(a, b, (((1,), (1,)), ((), ())), preferred_element_type=jnp.float32)


def nn_dot(a, b):
    return jnp.dot(a, b, preferred_element_type=jnp.float32)


def lanes(width):
    return lax.broadcasted_iota(jnp.int32, (1, width), 1)


def head_lanes(start):
    return (lanes(256) >= start) & (lanes(256) < start + HEAD)


def choose(queries, mine):
    return queries * jnp.where(mine, 1.0, 0.0).astype(jnp.bfloat16)


def count_in(values, free):
    one = jnp.where(lanes(256) == free, 1.0, 0.0)
    return values * (1.0 - one).astype(jnp.bfloat16) + one.astype(jnp.bfloat16)


def shuffle(forward):
    a = lax.broadcasted_iota(jnp.int32, (128, 128), 0)
    b = lax.broadcasted_iota(jnp.int32, (128, 128), 1)
    grouped, plain = (a, b) if forward else (b, a)
    source = ((grouped // 4) % 4) * 32 + (grouped // 16) * 4 + grouped % 4
    return jnp.where(source == plain, 1.0, 0.0).astype(jnp.bfloat16)


def kernel(
    tok, mod_in, w_in0, w_out0, w_in1, w_out1, out,
    mod, x, m, w, wo, q, k, v, first, stat, att, att_in, u, gathered,
    wt, wto, grouped, t, packed, mixed_t, r,
    load_sem, y_send, y_recv, s_send, s_recv, z_send, z_recv, a_send, a_recv,
    u_send, u_recv, g_send, g_recv, r_send, r_recv, own_sem, meet_sem,
):
    frame = lax.axis_index("frame")
    patch = lax.axis_index("patch")
    y = patch // 4
    z = (patch // 2) % 2
    core = patch % 2
    sibling = (frame, y * 4 + z * 2 + (1 - core))
    across = (frame, y * 4 + (1 - z) * 2 + core)

    def along(step):
        return (frame, ((y + step) % 4) * 4 + z * 2 + core)

    def peer_frame(step):
        return ((frame // 4 + step // 4) % 2) * 4 + (frame + step % 4) % 4

    def peer(step):
        return (peer_frame(step), patch)

    def beside_x(step):
        return ((frame // 4) * 4 + (frame + step) % 4, patch)

    opposite = ((frame + 4) % 8, patch)
    over_edge = ((frame + 4) % 8, y * 4 + (1 - z) * 2 + core)

    loads = [pltpu.make_async_copy(tok.at[y], x.at[0], load_sem.at[0])]
    for part in range(3):
        columns = pl.ds(pl.multiple_of(part * D + core * 512, 128), WIN)
        loads.append(
            pltpu.make_async_copy(w_in0.at[:, columns], w.at[:, pl.ds(part * WIN, WIN)], load_sem.at[1 + part])
        )
    loads.append(pltpu.make_async_copy(w_out0, wo, load_sem.at[4]))
    loads.append(pltpu.make_async_copy(w_in1, wt, load_sem.at[5]))
    loads.append(pltpu.make_async_copy(w_out1, wto, load_sem.at[6]))
    loads.append(pltpu.make_async_copy(mod_in, mod, load_sem.at[7]))
    for load in [loads[7]] + loads[:4]:
        load.start()

    barrier = pltpu.get_barrier_semaphore()
    beside = [beside_x(1), beside_x(3)]
    greeted = [sibling, across] + [along(s) for s in (1, 2, 3)] + beside + [over_edge]
    for device in greeted:
        pl.semaphore_signal(barrier, inc=1, device_id=device, device_id_type=MESH)
    loads[7].wait()
    table = [mod[part, 0:1, :] for part in range(3)]
    loads[0].wait()
    m[0, 0, 0] = modulate(x[0], table)
    pl.semaphore_wait(barrier, len(greeted))

    for device in beside + [across]:
        pl.semaphore_signal(meet_sem.at[0], inc=1, device_id=device, device_id_type=MESH)

    def remote(src, dst, send, recv, device):
        return pltpu.make_async_remote_copy(
            src_ref=src, dst_ref=dst, send_sem=send, recv_sem=recv, device_id=device, device_id_type=MESH
        )

    def rows_of(piece):
        return pl.ds(piece * 48, 48)

    def along_y(slot, piece):
        step = STEPS[slot]
        rows = rows_of(piece)
        return remote(
            tok.at[(y + 4 - step) % 4, rows], x.at[slot, rows],
            y_send.at[slot, piece], y_recv.at[slot, piece], along(4 - step),
        )

    def over_z(slot, piece):
        rows = rows_of(piece)
        return remote(
            m.at[0, slot, 0, rows], m.at[1, slot, 0, rows], z_send.at[slot, piece], z_recv.at[slot, piece], across
        )

    def to_sibling(half, slot, piece):
        rows = rows_of(piece)
        return remote(
            m.at[half, slot, 0, rows], m.at[half, slot, 1, rows],
            s_send.at[half, slot, piece], s_recv.at[half, slot, piece], sibling,
        )

    def arrive(slot, piece):
        along_y(slot, piece).wait_recv()
        rows = rows_of(piece)
        m[0, slot, 0, rows] = modulate(x[slot, rows], table)
        over_z(slot, piece).start()
        to_sibling(0, slot, piece).start()

    def pass_z(slot):
        for piece in range(2):
            over_z(slot, piece).wait_recv()
            to_sibling(1, slot, piece).start()

    def project(half, slot, count, quarters=(0, 1)):
        if 1 in quarters:
            for n in range(count):
                for piece in range(2):
                    to_sibling(half, slot + n, piece).wait_recv()
        chosen = slice(quarters[0], quarters[-1] + 1)
        mixed = m[half, slot : slot + count, chosen].reshape(96 * len(quarters) * count, D)
        flat = nn_dot(mixed, w[...] if half == 0 else w[:, WIN:])
        if half == 0:
            queries = (flat[:, :WIN] * SCALE).astype(jnp.bfloat16)
            flat = flat[:, WIN:]
        flat = flat.astype(jnp.bfloat16)
        for n in range(count):
            for index, quarter in enumerate(quarters):
                at = (n * len(quarters) + index) * 96
                if half == 0:
                    q[quarter, slot + n] = queries[at : at + 96].reshape(3, 32, WIN)
                rows = pl.ds(PLACES[half][slot + n] * 192 + quarter * 96, 96)
                k[rows, :] = flat[at : at + 96, :WIN]
                v[rows, :] = flat[at : at + 96, WIN:]

    for piece in range(2):
        along_y(1, piece).start()
        along_y(2, piece).start()
    for piece in range(2):
        over_z(0, piece).start()
        to_sibling(0, 0, piece).start()
    for load in loads[1:4]:
        load.wait()
    for load in loads[4:7]:
        load.start()
    project(0, 0, 1)
    arrive(1, 0)
    arrive(2, 0)
    for piece in range(2):
        along_y(1, piece).wait_send()
        along_y(3, piece).start()
    arrive(1, 1)
    arrive(2, 1)
    project(0, 1, 2, (0,))
    pass_z(0)
    project(0, 1, 2, (1,))
    project(1, 0, 1)
    pl.semaphore_wait(meet_sem.at[0], 3)
    pl.semaphore_signal(meet_sem.at[1], inc=1, device_id=opposite, device_id_type=MESH)

    def starts(j):
        return ((16 * j + 64 * core, 255), (16 * j + 72 + 64 * core, 0))

    def early(part, count):
        for j in range(4):
            window = slice(128 * j, 128 * j + 256)
            queries = q[part + (slice(None), slice(None), window)]
            shape = queries.shape[:3]
            queries, keys, values = queries.reshape(count, 256), k[:EARLY, window], v[:EARLY, window]
            for odd, (start, free) in enumerate(starts(j)):
                scores = nt_dot(choose(queries, head_lanes(start)), keys)
                top = jnp.max(scores, axis=-1, keepdims=True)
                weights = jnp.exp2(scores - top).astype(jnp.bfloat16)
                total = nn_dot(weights, count_in(values, free))
                first[(2 * j + odd,) + part] = total.reshape(shape + (256,))
                stat[(2 * j + odd,) + part] = jnp.broadcast_to(top, (count, 128)).reshape(shape + (128,))

    def late(g, j, carry):
        window = slice(128 * j, 128 * j + 256)
        queries = q[:, :, g, :, window].reshape(256, 256)
        keys, values = k[EARLY:, window], v[EARLY:, window]
        both = jnp.zeros((256, 256), jnp.float32)
        for odd, (start, free) in enumerate(starts(j)):
            h = 2 * j + odd
            mine = head_lanes(start)
            scores = nt_dot(choose(queries, mine), keys)
            parts = [scores[:, 128 * n : 128 * n + 128] for n in range(LATE // 128)]
            top = parts[0]
            for piece in parts[1:]:
                top = jnp.maximum(top, piece)
            before = stat[h, :, :, g].reshape(256, 128)
            top = jnp.maximum(before, jnp.max(top, axis=-1, keepdims=True))
            weights = jnp.concatenate([jnp.exp2(piece - top).astype(jnp.bfloat16) for piece in parts], axis=1)
            part = nn_dot(weights, count_in(values, free))
            shrink = jnp.exp2(before - top)
            earlier = first[h, :, :, g].reshape(256, 256)
            total = jnp.concatenate(
                [part[:, :128] + earlier[:, :128] * shrink, part[:, 128:] + earlier[:, 128:] * shrink], axis=1
            )
            both = jnp.where(mine, total * (1.0 / total[:, free : free + 1]), both)
        att[g, :, 128 * j : 128 * j + 128] = (carry + both[:, :128]).astype(jnp.bfloat16)
        if j == 3:
            att[g, :, 512:] = both[:, 128:].astype(jnp.bfloat16)
        return both[:, 128:]

    def swap(g):
        return remote(att.at[g, pl.ds(128, 128)], att_in.at[g], a_send.at[g], a_recv.at[g], sibling)

    def give(g, slot):
        return remote(u.at[g, slot], gathered.at[g, y], u_send.at[g, slot], u_recv.at[g, slot], along(STEPS[slot]))

    def own_give(g):
        return pltpu.make_async_copy(u.at[g, 0], gathered.at[g, y], own_sem.at[0, g])

    def finish(g):
        swap(g).wait_recv()
        mine = pl.ds(pl.multiple_of(core * 512, 128), WIN)
        other = pl.ds(pl.multiple_of((1 - core) * 512, 128), WIN)
        flat = nn_dot(att[g, :128], wo[mine, :]) + nn_dot(att_in[g], wo[other, :])
        values = x[:, pl.ds(pl.multiple_of(g * 32, 32), 32), :].astype(jnp.float32)
        u[g] = (values + table[2] * flat.reshape(4, 32, D)).astype(jnp.bfloat16)
        for slot in range(1, 4):
            give(g, slot).start()
        own_give(g).start()

    early((0, slice(0, 3)), 288)
    arrive(3, 0)
    arrive(3, 1)
    early((1, slice(0, 3)), 288)
    project(0, 3, 1)
    pass_z(1)
    pass_z(2)
    early((slice(0, 2), 3), 192)
    project(1, 1, 2)
    pass_z(3)
    project(1, 3, 1)
    loads[4].wait()

    def turn(g, carry):
        edge = jnp.zeros((256, 128), jnp.float32)
        edge = late(g, 0, edge)
        edge = late(g, 1, edge)

        @pl.when(g > 0)
        def _():
            finish(g - 1)

        edge = late(g, 2, edge)
        late(g, 3, edge)
        swap(g).start()
        return carry

    lax.fori_loop(0, 3, turn, 0)

    def spread(g, step):
        return remote(
            grouped.at[g, peer_frame(step)], t.at[g, frame], g_send.at[g, step], g_recv.at[g, step], peer(step)
        )

    def own_spread(g):
        return pltpu.make_async_copy(grouped.at[g, frame], t.at[g, frame], own_sem.at[1, g])

    def collect(g, step):
        return remote(r.at[g, peer_frame(step)], out.at[g, frame], r_send.at[g, step], r_recv.at[g, step], peer(step))

    def own_collect(g):
        return pltpu.make_async_copy(r.at[g, frame], out.at[g, frame], own_sem.at[2, g])

    forward = shuffle(True)
    pl.semaphore_wait(meet_sem.at[1], 1)

    def relay(g, carry):
        own_give(g).wait()
        for slot in range(1, 4):
            give(g, slot).wait_recv()
        grouped[g] = nn_dot(forward, gathered[g].reshape(128, D)).astype(jnp.bfloat16).reshape(8, 16, D)
        for step in FAR_FIRST:
            spread(g, step).start()
        own_spread(g).start()
        return carry

    relay(0, 0)
    finish(2)
    lax.fori_loop(1, 3, relay, 0)
    loads[5].wait()
    loads[6].wait()

    a = lax.broadcasted_iota(jnp.int32, (128, 128), 0)
    b = lax.broadcasted_iota(jnp.int32, (128, 128), 1)
    bias = jnp.where(a % 4 == b % 4, 0.0, -1e30)
    table1 = [mod[part, 1:2, :] for part in range(3)]

    def block(g, carry):
        own_spread(g).wait()
        for step in range(1, 8):
            spread(g, step).wait_recv()
        values = t[g].reshape(128, D)
        mixed = modulate(values, table1)
        packed[:, :D] = (nn_dot(mixed, wt[:, :D]) * SCALE).astype(jnp.bfloat16)
        packed[:, D : 2 * D] = nn_dot(mixed, wt[:, D : 2 * D]).astype(jnp.bfloat16)
        packed[:, 2 * D :] = nn_dot(mixed, wt[:, 2 * D :]).astype(jnp.bfloat16)
        spots = []
        scores = []
        for h in range(HEADS):
            at = 128 * min(HEAD * h // 128, 7)
            start = HEAD * h - at
            spots.append((at, head_lanes(start), 0 if start else 255))
            queries = choose(packed[:, at : at + 256], spots[h][1])
            scores.append(nt_dot(queries, packed[:, D + at : D + at + 256]) + bias)
        weights = []
        for h in range(HEADS):
            top = jnp.max(scores[h], axis=-1, keepdims=True)
            weights.append(jnp.exp2(scores[h] - top).astype(jnp.bfloat16))
        tiles = [None] * 9
        for h, (at, mine, free) in enumerate(spots):
            part = nn_dot(weights[h], count_in(packed[:, 2 * D + at : 2 * D + at + 256], free))
            part = jnp.where(mine, part * (1.0 / part[:, free : free + 1]), 0.0)
            for side in range(2):
                tile = at // 128 + side
                piece = part[:, 128 * side : 128 * side + 128]
                tiles[tile] = piece if tiles[tile] is None else tiles[tile] + piece
        for tile in range(9):
            mixed_t[:, 128 * tile : 128 * tile + 128] = tiles[tile].astype(jnp.bfloat16)
        flat = nn_dot(mixed_t[...], wto[...])
        r[g] = (values.astype(jnp.float32) + table1[2] * flat).astype(jnp.bfloat16).reshape(8, 16, D)
        for step in FAR_FIRST:
            collect(g, step).start()
        own_collect(g).start()
        return carry

    lax.fori_loop(0, 3, block, 0)

    def settle(g, carry):
        own_collect(g).wait()
        for step in range(1, 8):
            collect(g, step).wait_recv()
        return carry

    lax.fori_loop(0, 3, settle, 0)

    for piece in range(2):
        along_y(2, piece).wait_send()
        along_y(3, piece).wait_send()
        for slot in range(4):
            over_z(slot, piece).wait_send()
            to_sibling(0, slot, piece).wait_send()
            to_sibling(1, slot, piece).wait_send()

    def drain(g, carry):
        swap(g).wait_send()
        for slot in range(1, 4):
            give(g, slot).wait_send()
        for step in range(1, 8):
            spread(g, step).wait_send()
            collect(g, step).wait_send()
        return carry

    lax.fori_loop(0, 3, drain, 0)


def reorder(back, out):
    backward = shuffle(False)
    for g in range(3):
        rows = nn_dot(backward, back[g].reshape(128, D)).astype(jnp.bfloat16)
        out[:, g * 32 : g * 32 + 32, :] = rows.reshape(4, 32, D)


def shards(tokens, modulation, spatial_input, spatial_output, temporal_input, temporal_output):
    dma = pltpu.SemaphoreType.DMA
    held = pl.BlockSpec(memory_space=pl.ANY)

    def bf16(*shape):
        return pltpu.VMEM(shape, jnp.bfloat16)

    back = pl.pallas_call(
        kernel,
        out_shape=jax.ShapeDtypeStruct((3, 8, 16, D), jnp.bfloat16),
        in_specs=[held] * 6,
        out_specs=held,
        scratch_shapes=[
            pltpu.VMEM((3, 2, D), jnp.float32),
            bf16(4, 96, D),
            bf16(2, 4, 2, 96, D),
            bf16(D, 3 * WIN),
            bf16(D, D),
            bf16(2, 4, 3, 32, WIN),
            bf16(1536, WIN),
            bf16(1536, WIN),
            pltpu.VMEM((8, 2, 4, 3, 32, 256), jnp.float32),
            pltpu.VMEM((8, 2, 4, 3, 32, 128), jnp.float32),
            bf16(3, 256, WIN),
            bf16(3, 128, WIN),
            bf16(3, 4, 32, D),
            bf16(3, 4, 32, D),
            bf16(D, 3 * D),
            bf16(D, D),
            bf16(3, 8, 16, D),
            bf16(3, 8, 16, D),
            bf16(128, 3 * D),
            bf16(128, D),
            bf16(3, 8, 16, D),
            dma((8,)),
            dma((4, 2)), dma((4, 2)),
            dma((2, 4, 2)), dma((2, 4, 2)),
            dma((4, 2)), dma((4, 2)),
            dma((3,)), dma((3,)),
            dma((3, 4)), dma((3, 4)),
            dma((3, 8)), dma((3, 8)),
            dma((3, 8)), dma((3, 8)),
            dma((3, 3)),
            pltpu.SemaphoreType.REGULAR((2,)),
        ],
        compiler_params=pltpu.CompilerParams(
            collective_id=0, has_side_effects=True, vmem_limit_bytes=VMEM_LIMIT
        ),
        name="block_pair",
    )(tokens, jnp.transpose(modulation, (1, 0, 2)), spatial_input, spatial_output, temporal_input, temporal_output)
    vmem = pl.BlockSpec(memory_space=pltpu.VMEM)
    return pl.pallas_call(
        reorder,
        out_shape=jax.ShapeDtypeStruct((4, 96, D), jnp.bfloat16),
        in_specs=[vmem],
        out_specs=vmem,
        compiler_params=pltpu.CompilerParams(vmem_limit_bytes=VMEM_LIMIT),
        name="reorder",
    )(back)


def solution(mesh):
    in_specs = (P("frame", "patch", None), P(), P(), P(), P(), P())
    out_specs = P("frame", "patch", None)
    return jax.shard_map(shards, mesh=mesh, in_specs=in_specs, out_specs=out_specs, check_vma=False)
```

```python
import math

import jax
import jax.numpy as jnp
from jax import lax
from jax.experimental import pallas as pl
from jax.experimental.pallas import tpu as pltpu
from jax.sharding import PartitionSpec as P

D = 1152
HEADS = 16
HEAD = 72
WIN = 640
EARLY = 768
LATE = 768
PLACES = ((0, 1, 2, 4), (3, 5, 6, 7))
SCALE = math.log2(math.e) / math.sqrt(HEAD)
MESH = pl.DeviceIdType.MESH
VMEM_LIMIT = 60 * 1024 * 1024
FAR_FIRST = (6, 5, 2, 7, 1, 4, 3)
STEPS = (0, 1, 3, 2)


def modulate(values, table):
    wide = values.astype(jnp.float32)
    centre = jnp.mean(wide, axis=-1, keepdims=True)
    wide = wide - centre
    spread = jnp.mean(jnp.square(wide), axis=-1, keepdims=True)
    normed = wide * lax.rsqrt(spread + 1e-06)
    return (normed * (1.0 + table[1]) + table[0]).astype(jnp.bfloat16)


def nt_dot(a, b):
    return lax.dot_general(a, b, (((1,), (1,)), ((), ())), preferred_element_type=jnp.float32)


def nn_dot(a, b):
    return jnp.dot(a, b, preferred_element_type=jnp.float32)


def lanes(width):
    return lax.broadcasted_iota(jnp.int32, (1, width), 1)


def head_lanes(start):
    return (lanes(256) >= start) & (lanes(256) < start + HEAD)


def choose(queries, mine):
    return queries * jnp.where(mine, 1.0, 0.0).astype(jnp.bfloat16)


def count_in(values, free):
    one = jnp.where(lanes(256) == free, 1.0, 0.0)
    return values * (1.0 - one).astype(jnp.bfloat16) + one.astype(jnp.bfloat16)


def shuffle(forward):
    a = lax.broadcasted_iota(jnp.int32, (128, 128), 0)
    b = lax.broadcasted_iota(jnp.int32, (128, 128), 1)
    grouped, plain = (a, b) if forward else (b, a)
    source = ((grouped // 4) % 4) * 32 + (grouped // 16) * 4 + grouped % 4
    return jnp.where(source == plain, 1.0, 0.0).astype(jnp.bfloat16)


def kernel(
    tok, mod_in, w_in0, w_out0, w_in1, w_out1, out,
    mod, x, m, w, wo, q, k, v, first, stat, att, att_in, u, gathered,
    wt, wto, grouped, t, packed, mixed_t, r,
    load_sem, y_send, y_recv, s_send, s_recv, z_send, z_recv, a_send, a_recv,
    u_send, u_recv, g_send, g_recv, r_send, r_recv, own_sem, meet_sem,
):
    frame = lax.axis_index("frame")
    patch = lax.axis_index("patch")
    y = patch // 4
    z = (patch // 2) % 2
    core = patch % 2
    sibling = (frame, y * 4 + z * 2 + (1 - core))
    across = (frame, y * 4 + (1 - z) * 2 + core)

    def along(step):
        return (frame, ((y + step) % 4) * 4 + z * 2 + core)

    def peer_frame(step):
        return ((frame // 4 + step // 4) % 2) * 4 + (frame + step % 4) % 4

    def peer(step):
        return (peer_frame(step), patch)

    def beside_x(step):
        return ((frame // 4) * 4 + (frame + step) % 4, patch)

    opposite = ((frame + 4) % 8, patch)
    over_edge = ((frame + 4) % 8, y * 4 + (1 - z) * 2 + core)

    loads = [pltpu.make_async_copy(tok.at[y], x.at[0], load_sem.at[0])]
    for part in range(3):
        columns = pl.ds(pl.multiple_of(part * D + core * 512, 128), WIN)
        loads.append(
            pltpu.make_async_copy(w_in0.at[:, columns], w.at[:, pl.ds(part * WIN, WIN)], load_sem.at[1 + part])
        )
    loads.append(pltpu.make_async_copy(w_out0, wo, load_sem.at[4]))
    loads.append(pltpu.make_async_copy(w_in1, wt, load_sem.at[5]))
    loads.append(pltpu.make_async_copy(w_out1, wto, load_sem.at[6]))
    loads.append(pltpu.make_async_copy(mod_in, mod, load_sem.at[7]))
    for load in [loads[7]] + loads[:4]:
        load.start()

    barrier = pltpu.get_barrier_semaphore()
    beside = [beside_x(1), beside_x(3)]
    greeted = [sibling, across] + [along(s) for s in (1, 2, 3)] + beside + [over_edge]
    for device in greeted:
        pl.semaphore_signal(barrier, inc=1, device_id=device, device_id_type=MESH)
    loads[7].wait()
    table = [mod[part, 0:1, :] for part in range(3)]
    loads[0].wait()
    m[0, 0, 0] = modulate(x[0], table)
    pl.semaphore_wait(barrier, len(greeted))

    for device in beside + [across]:
        pl.semaphore_signal(meet_sem.at[0], inc=1, device_id=device, device_id_type=MESH)

    def remote(src, dst, send, recv, device):
        return pltpu.make_async_remote_copy(
            src_ref=src, dst_ref=dst, send_sem=send, recv_sem=recv, device_id=device, device_id_type=MESH
        )

    def rows_of(piece):
        return pl.ds(piece * 48, 48)

    def along_y(slot, piece):
        step = STEPS[slot]
        rows = rows_of(piece)
        return remote(
            tok.at[(y + 4 - step) % 4, rows], x.at[slot, rows],
            y_send.at[slot, piece], y_recv.at[slot, piece], along(4 - step),
        )

    def over_z(slot, piece):
        rows = rows_of(piece)
        return remote(
            m.at[0, slot, 0, rows], m.at[1, slot, 0, rows], z_send.at[slot, piece], z_recv.at[slot, piece], across
        )

    def to_sibling(half, slot, piece):
        rows = rows_of(piece)
        return remote(
            m.at[half, slot, 0, rows], m.at[half, slot, 1, rows],
            s_send.at[half, slot, piece], s_recv.at[half, slot, piece], sibling,
        )

    def arrive(slot, piece):
        along_y(slot, piece).wait_recv()
        rows = rows_of(piece)
        m[0, slot, 0, rows] = modulate(x[slot, rows], table)
        over_z(slot, piece).start()
        to_sibling(0, slot, piece).start()

    def pass_z(slot):
        for piece in range(2):
            over_z(slot, piece).wait_recv()
            to_sibling(1, slot, piece).start()

    def project(half, slot, count, quarters=(0, 1)):
        if 1 in quarters:
            for n in range(count):
                for piece in range(2):
                    to_sibling(half, slot + n, piece).wait_recv()
        chosen = slice(quarters[0], quarters[-1] + 1)
        mixed = m[half, slot : slot + count, chosen].reshape(96 * len(quarters) * count, D)
        flat = nn_dot(mixed, w[...] if half == 0 else w[:, WIN:])
        if half == 0:
            queries = (flat[:, :WIN] * SCALE).astype(jnp.bfloat16)
            flat = flat[:, WIN:]
        flat = flat.astype(jnp.bfloat16)
        for n in range(count):
            for index, quarter in enumerate(quarters):
                at = (n * len(quarters) + index) * 96
                if half == 0:
                    q[quarter, slot + n] = queries[at : at + 96].reshape(3, 32, WIN)
                rows = pl.ds(PLACES[half][slot + n] * 192 + quarter * 96, 96)
                k[rows, :] = flat[at : at + 96, :WIN]
                v[rows, :] = flat[at : at + 96, WIN:]

    for piece in range(2):
        along_y(1, piece).start()
        along_y(2, piece).start()
    for piece in range(2):
        over_z(0, piece).start()
        to_sibling(0, 0, piece).start()
    for load in loads[1:4]:
        load.wait()
    for load in loads[4:7]:
        load.start()
    project(0, 0, 1)
    arrive(1, 0)
    arrive(2, 0)
    for piece in range(2):
        along_y(3, piece).start()
    arrive(1, 1)
    arrive(2, 1)
    project(0, 1, 2, (0,))
    pass_z(0)
    project(0, 1, 2, (1,))
    project(1, 0, 1)
    pl.semaphore_wait(meet_sem.at[0], 3)
    pl.semaphore_signal(meet_sem.at[1], inc=1, device_id=opposite, device_id_type=MESH)

    def starts(j):
        return ((16 * j + 64 * core, 255), (16 * j + 72 + 64 * core, 0))

    def early(part, count):
        for j in range(4):
            window = slice(128 * j, 128 * j + 256)
            queries = q[part + (slice(None), slice(None), window)]
            shape = queries.shape[:3]
            queries, keys, values = queries.reshape(count, 256), k[:EARLY, window], v[:EARLY, window]
            for odd, (start, free) in enumerate(starts(j)):
                scores = nt_dot(choose(queries, head_lanes(start)), keys)
                top = jnp.max(scores, axis=-1, keepdims=True)
                weights = jnp.exp2(scores - top).astype(jnp.bfloat16)
                total = nn_dot(weights, count_in(values, free))
                first[(2 * j + odd,) + part] = total.reshape(shape + (256,))
                stat[(2 * j + odd,) + part] = jnp.broadcast_to(top, (count, 128)).reshape(shape + (128,))

    def late(g, j, carry):
        window = slice(128 * j, 128 * j + 256)
        queries = q[:, :, g, :, window].reshape(256, 256)
        keys, values = k[EARLY:, window], v[EARLY:, window]
        both = jnp.zeros((256, 256), jnp.float32)
        for odd, (start, free) in enumerate(starts(j)):
            h = 2 * j + odd
            mine = head_lanes(start)
            scores = nt_dot(choose(queries, mine), keys)
            parts = [scores[:, 128 * n : 128 * n + 128] for n in range(LATE // 128)]
            top = parts[0]
            for piece in parts[1:]:
                top = jnp.maximum(top, piece)
            before = stat[h, :, :, g].reshape(256, 128)
            top = jnp.maximum(before, jnp.max(top, axis=-1, keepdims=True))
            weights = jnp.concatenate([jnp.exp2(piece - top).astype(jnp.bfloat16) for piece in parts], axis=1)
            part = nn_dot(weights, count_in(values, free))
            shrink = jnp.exp2(before - top)
            earlier = first[h, :, :, g].reshape(256, 256)
            total = jnp.concatenate(
                [part[:, :128] + earlier[:, :128] * shrink, part[:, 128:] + earlier[:, 128:] * shrink], axis=1
            )
            both = jnp.where(mine, total * (1.0 / total[:, free : free + 1]), both)
        att[g, :, 128 * j : 128 * j + 128] = (carry + both[:, :128]).astype(jnp.bfloat16)
        if j == 3:
            att[g, :, 512:] = both[:, 128:].astype(jnp.bfloat16)
        return both[:, 128:]

    def swap(g):
        return remote(att.at[g, pl.ds(128, 128)], att_in.at[g], a_send.at[g], a_recv.at[g], sibling)

    def give(g, slot):
        return remote(u.at[g, slot], gathered.at[g, y], u_send.at[g, slot], u_recv.at[g, slot], along(STEPS[slot]))

    def own_give(g):
        return pltpu.make_async_copy(u.at[g, 0], gathered.at[g, y], own_sem.at[0, g])

    def finish(g):
        swap(g).wait_recv()
        mine = pl.ds(pl.multiple_of(core * 512, 128), WIN)
        other = pl.ds(pl.multiple_of((1 - core) * 512, 128), WIN)
        flat = nn_dot(att[g, :128], wo[mine, :]) + nn_dot(att_in[g], wo[other, :])
        values = x[:, pl.ds(pl.multiple_of(g * 32, 32), 32), :].astype(jnp.float32)
        u[g] = (values + table[2] * flat.reshape(4, 32, D)).astype(jnp.bfloat16)
        for slot in range(1, 4):
            give(g, slot).start()
        own_give(g).start()

    arrive(3, 0)
    arrive(3, 1)
    early((0, slice(0, 3)), 288)
    early((1, slice(0, 3)), 288)
    project(0, 3, 1)
    pass_z(1)
    pass_z(2)
    early((slice(0, 2), 3), 192)
    project(1, 1, 2)
    pass_z(3)
    project(1, 3, 1)
    loads[4].wait()

    def turn(g, carry):
        edge = jnp.zeros((256, 128), jnp.float32)
        edge = late(g, 0, edge)
        edge = late(g, 1, edge)

        @pl.when(g > 0)
        def _():
            finish(g - 1)

        edge = late(g, 2, edge)
        late(g, 3, edge)
        swap(g).start()
        return carry

    lax.fori_loop(0, 3, turn, 0)

    def spread(g, step):
        return remote(
            grouped.at[g, peer_frame(step)], t.at[g, frame], g_send.at[g, step], g_recv.at[g, step], peer(step)
        )

    def own_spread(g):
        return pltpu.make_async_copy(grouped.at[g, frame], t.at[g, frame], own_sem.at[1, g])

    def collect(g, step):
        return remote(r.at[g, peer_frame(step)], out.at[g, frame], r_send.at[g, step], r_recv.at[g, step], peer(step))

    def own_collect(g):
        return pltpu.make_async_copy(r.at[g, frame], out.at[g, frame], own_sem.at[2, g])

    forward = shuffle(True)
    pl.semaphore_wait(meet_sem.at[1], 1)

    def relay(g, carry):
        own_give(g).wait()
        for slot in range(1, 4):
            give(g, slot).wait_recv()
        grouped[g] = nn_dot(forward, gathered[g].reshape(128, D)).astype(jnp.bfloat16).reshape(8, 16, D)
        for step in FAR_FIRST:
            spread(g, step).start()
        own_spread(g).start()
        return carry

    relay(0, 0)
    finish(2)
    lax.fori_loop(1, 3, relay, 0)
    loads[5].wait()
    loads[6].wait()

    a = lax.broadcasted_iota(jnp.int32, (128, 128), 0)
    b = lax.broadcasted_iota(jnp.int32, (128, 128), 1)
    bias = jnp.where(a % 4 == b % 4, 0.0, -1e30)
    table1 = [mod[part, 1:2, :] for part in range(3)]

    def block(g, carry):
        own_spread(g).wait()
        for step in range(1, 8):
            spread(g, step).wait_recv()
        values = t[g].reshape(128, D)
        mixed = modulate(values, table1)
        packed[:, :D] = (nn_dot(mixed, wt[:, :D]) * SCALE).astype(jnp.bfloat16)
        packed[:, D : 2 * D] = nn_dot(mixed, wt[:, D : 2 * D]).astype(jnp.bfloat16)
        packed[:, 2 * D :] = nn_dot(mixed, wt[:, 2 * D :]).astype(jnp.bfloat16)
        spots = []
        scores = []
        for h in range(HEADS):
            at = 128 * min(HEAD * h // 128, 7)
            start = HEAD * h - at
            spots.append((at, head_lanes(start), 0 if start else 255))
            queries = choose(packed[:, at : at + 256], spots[h][1])
            scores.append(nt_dot(queries, packed[:, D + at : D + at + 256]) + bias)
        weights = []
        for h in range(HEADS):
            top = jnp.max(scores[h], axis=-1, keepdims=True)
            weights.append(jnp.exp2(scores[h] - top).astype(jnp.bfloat16))
        tiles = [None] * 9
        for h, (at, mine, free) in enumerate(spots):
            part = nn_dot(weights[h], count_in(packed[:, 2 * D + at : 2 * D + at + 256], free))
            part = jnp.where(mine, part * (1.0 / part[:, free : free + 1]), 0.0)
            for side in range(2):
                tile = at // 128 + side
                piece = part[:, 128 * side : 128 * side + 128]
                tiles[tile] = piece if tiles[tile] is None else tiles[tile] + piece
        for tile in range(9):
            mixed_t[:, 128 * tile : 128 * tile + 128] = tiles[tile].astype(jnp.bfloat16)
        flat = nn_dot(mixed_t[...], wto[...])
        r[g] = (values.astype(jnp.float32) + table1[2] * flat).astype(jnp.bfloat16).reshape(8, 16, D)
        for step in FAR_FIRST:
            collect(g, step).start()
        own_collect(g).start()
        return carry

    lax.fori_loop(0, 3, block, 0)

    def settle(g, carry):
        own_collect(g).wait()
        for step in range(1, 8):
            collect(g, step).wait_recv()
        return carry

    lax.fori_loop(0, 3, settle, 0)

    for piece in range(2):
        along_y(1, piece).wait_send()
        along_y(2, piece).wait_send()
        along_y(3, piece).wait_send()
        for slot in range(4):
            over_z(slot, piece).wait_send()
            to_sibling(0, slot, piece).wait_send()
            to_sibling(1, slot, piece).wait_send()

    def drain(g, carry):
        swap(g).wait_send()
        for slot in range(1, 4):
            give(g, slot).wait_send()
        for step in range(1, 8):
            spread(g, step).wait_send()
            collect(g, step).wait_send()
        return carry

    lax.fori_loop(0, 3, drain, 0)


def reorder(back, out):
    rows = nn_dot(shuffle(False), back[0].reshape(128, D)).astype(jnp.bfloat16)
    out[...] = rows.reshape(4, 32, D)


def shards(tokens, modulation, spatial_input, spatial_output, temporal_input, temporal_output):
    dma = pltpu.SemaphoreType.DMA
    held = pl.BlockSpec(memory_space=pl.ANY)

    def bf16(*shape):
        return pltpu.VMEM(shape, jnp.bfloat16)

    back = pl.pallas_call(
        kernel,
        out_shape=jax.ShapeDtypeStruct((3, 8, 16, D), jnp.bfloat16),
        in_specs=[held] * 6,
        out_specs=held,
        scratch_shapes=[
            pltpu.VMEM((3, 2, D), jnp.float32),
            bf16(4, 96, D),
            bf16(2, 4, 2, 96, D),
            bf16(D, 3 * WIN),
            bf16(D, D),
            bf16(2, 4, 3, 32, WIN),
            bf16(1536, WIN),
            bf16(1536, WIN),
            pltpu.VMEM((8, 2, 4, 3, 32, 256), jnp.float32),
            pltpu.VMEM((8, 2, 4, 3, 32, 128), jnp.float32),
            bf16(3, 256, WIN),
            bf16(3, 128, WIN),
            bf16(3, 4, 32, D),
            bf16(3, 4, 32, D),
            bf16(D, 3 * D),
            bf16(D, D),
            bf16(3, 8, 16, D),
            bf16(3, 8, 16, D),
            bf16(128, 3 * D),
            bf16(128, D),
            bf16(3, 8, 16, D),
            dma((8,)),
            dma((4, 2)), dma((4, 2)),
            dma((2, 4, 2)), dma((2, 4, 2)),
            dma((4, 2)), dma((4, 2)),
            dma((3,)), dma((3,)),
            dma((3, 4)), dma((3, 4)),
            dma((3, 8)), dma((3, 8)),
            dma((3, 8)), dma((3, 8)),
            dma((3, 3)),
            pltpu.SemaphoreType.REGULAR((2,)),
        ],
        compiler_params=pltpu.CompilerParams(
            collective_id=0, has_side_effects=True, vmem_limit_bytes=VMEM_LIMIT
        ),
        name="block_pair",
    )(tokens, jnp.transpose(modulation, (1, 0, 2)), spatial_input, spatial_output, temporal_input, temporal_output)
    return pl.pallas_call(
        reorder,
        out_shape=jax.ShapeDtypeStruct((4, 96, D), jnp.bfloat16),
        grid=(3,),
        in_specs=[pl.BlockSpec((1, 8, 16, D), lambda g: (g, 0, 0, 0))],
        out_specs=pl.BlockSpec((4, 32, D), lambda g: (0, g, 0)),
        compiler_params=pltpu.CompilerParams(vmem_limit_bytes=VMEM_LIMIT),
        name="reorder",
    )(back)


def solution(mesh):
    in_specs = (P("frame", "patch", None), P(), P(), P(), P(), P())
    out_specs = P("frame", "patch", None)
    return jax.shard_map(shards, mesh=mesh, in_specs=in_specs, out_specs=out_specs, check_vma=False)
```

```python
import math

import jax
import jax.numpy as jnp
from jax import lax
from jax.experimental import pallas as pl
from jax.experimental.pallas import tpu as pltpu
from jax.sharding import PartitionSpec as P

D = 1152
HEADS = 16
HEAD = 72
WIN = 640
EARLY = 768
LATE = 768
PLACES = ((0, 1, 2, 4), (3, 5, 6, 7))
SCALE = math.log2(math.e) / math.sqrt(HEAD)
MESH = pl.DeviceIdType.MESH
VMEM_LIMIT = 60 * 1024 * 1024
FAR_FIRST = (6, 5, 2, 7, 1, 4, 3)
STEPS = (0, 1, 3, 2)


def modulate(values, table):
    wide = values.astype(jnp.float32)
    centre = jnp.mean(wide, axis=-1, keepdims=True)
    wide = wide - centre
    spread = jnp.mean(jnp.square(wide), axis=-1, keepdims=True)
    normed = wide * lax.rsqrt(spread + 1e-06)
    return (normed * (1.0 + table[1]) + table[0]).astype(jnp.bfloat16)


def nt_dot(a, b):
    return lax.dot_general(a, b, (((1,), (1,)), ((), ())), preferred_element_type=jnp.float32)


def nn_dot(a, b):
    return jnp.dot(a, b, preferred_element_type=jnp.float32)


def lanes(width):
    return lax.broadcasted_iota(jnp.int32, (1, width), 1)


def head_lanes(start):
    return (lanes(256) >= start) & (lanes(256) < start + HEAD)


def choose(queries, mine):
    return queries * jnp.where(mine, 1.0, 0.0).astype(jnp.bfloat16)


def count_in(values, free):
    one = jnp.where(lanes(256) == free, 1.0, 0.0)
    return values * (1.0 - one).astype(jnp.bfloat16) + one.astype(jnp.bfloat16)


def shuffle(forward):
    a = lax.broadcasted_iota(jnp.int32, (128, 128), 0)
    b = lax.broadcasted_iota(jnp.int32, (128, 128), 1)
    grouped, plain = (a, b) if forward else (b, a)
    source = ((grouped // 4) % 4) * 32 + (grouped // 16) * 4 + grouped % 4
    return jnp.where(source == plain, 1.0, 0.0).astype(jnp.bfloat16)


def kernel(
    tok, mod_in, w_in0, w_out0, w_in1, w_out1, out,
    mod, x, m, w, wo, q, k, v, first, stat, att, att_in, u, gathered,
    wt, wto, grouped, t, packed, mixed_t, r,
    load_sem, y_send, y_recv, s_send, s_recv, z_send, z_recv, a_send, a_recv,
    u_send, u_recv, g_send, g_recv, r_send, r_recv, own_sem, meet_sem,
):
    frame = lax.axis_index("frame")
    patch = lax.axis_index("patch")
    y = patch // 4
    z = (patch // 2) % 2
    core = patch % 2
    sibling = (frame, y * 4 + z * 2 + (1 - core))
    across = (frame, y * 4 + (1 - z) * 2 + core)

    def along(step):
        return (frame, ((y + step) % 4) * 4 + z * 2 + core)

    def peer_frame(step):
        return ((frame // 4 + step // 4) % 2) * 4 + (frame + step % 4) % 4

    def peer(step):
        return (peer_frame(step), patch)

    def beside_x(step):
        return ((frame // 4) * 4 + (frame + step) % 4, patch)

    opposite = ((frame + 4) % 8, patch)
    over_edge = ((frame + 4) % 8, y * 4 + (1 - z) * 2 + core)

    loads = [pltpu.make_async_copy(tok.at[y], x.at[0], load_sem.at[0])]
    for part in range(3):
        columns = pl.ds(pl.multiple_of(part * D + core * 512, 128), WIN)
        loads.append(
            pltpu.make_async_copy(w_in0.at[:, columns], w.at[:, pl.ds(part * WIN, WIN)], load_sem.at[1 + part])
        )
    loads.append(pltpu.make_async_copy(w_out0, wo, load_sem.at[4]))
    loads.append(pltpu.make_async_copy(w_in1, wt, load_sem.at[5]))
    loads.append(pltpu.make_async_copy(w_out1, wto, load_sem.at[6]))
    loads.append(pltpu.make_async_copy(mod_in, mod, load_sem.at[7]))
    for load in [loads[7]] + loads[:4]:
        load.start()

    barrier = pltpu.get_barrier_semaphore()
    beside = [beside_x(1), beside_x(3)]
    greeted = [sibling, across] + [along(s) for s in (1, 2, 3)] + beside + [over_edge]
    for device in greeted:
        pl.semaphore_signal(barrier, inc=1, device_id=device, device_id_type=MESH)
    loads[7].wait()
    table = [mod[part, 0:1, :] for part in range(3)]
    loads[0].wait()
    m[0, 0, 0] = modulate(x[0], table)
    pl.semaphore_wait(barrier, len(greeted))

    for device in beside + [across]:
        pl.semaphore_signal(meet_sem.at[0], inc=1, device_id=device, device_id_type=MESH)

    def remote(src, dst, send, recv, device):
        return pltpu.make_async_remote_copy(
            src_ref=src, dst_ref=dst, send_sem=send, recv_sem=recv, device_id=device, device_id_type=MESH
        )

    def rows_of(piece):
        return pl.ds(piece * 48, 48)

    def along_y(slot, piece):
        step = STEPS[slot]
        rows = rows_of(piece)
        return remote(
            tok.at[(y + 4 - step) % 4, rows], x.at[slot, rows],
            y_send.at[slot, piece], y_recv.at[slot, piece], along(4 - step),
        )

    def over_z(slot, piece):
        rows = rows_of(piece)
        return remote(
            m.at[0, slot, 0, rows], m.at[1, slot, 0, rows], z_send.at[slot, piece], z_recv.at[slot, piece], across
        )

    def to_sibling(half, slot, piece):
        rows = rows_of(piece)
        return remote(
            m.at[half, slot, 0, rows], m.at[half, slot, 1, rows],
            s_send.at[half, slot, piece], s_recv.at[half, slot, piece], sibling,
        )

    def arrive(slot, piece):
        along_y(slot, piece).wait_recv()
        rows = rows_of(piece)
        m[0, slot, 0, rows] = modulate(x[slot, rows], table)
        over_z(slot, piece).start()
        to_sibling(0, slot, piece).start()

    def pass_z(slot):
        for piece in range(2):
            over_z(slot, piece).wait_recv()
            to_sibling(1, slot, piece).start()

    def project(half, slot, count, quarters=(0, 1)):
        if 1 in quarters:
            for n in range(count):
                for piece in range(2):
                    to_sibling(half, slot + n, piece).wait_recv()
        chosen = slice(quarters[0], quarters[-1] + 1)
        mixed = m[half, slot : slot + count, chosen].reshape(96 * len(quarters) * count, D)
        flat = nn_dot(mixed, w[...] if half == 0 else w[:, WIN:])
        if half == 0:
            queries = (flat[:, :WIN] * SCALE).astype(jnp.bfloat16)
            flat = flat[:, WIN:]
        flat = flat.astype(jnp.bfloat16)
        for n in range(count):
            for index, quarter in enumerate(quarters):
                at = (n * len(quarters) + index) * 96
                if half == 0:
                    q[quarter, slot + n] = queries[at : at + 96].reshape(3, 32, WIN)
                rows = pl.ds(PLACES[half][slot + n] * 192 + quarter * 96, 96)
                k[rows, :] = flat[at : at + 96, :WIN]
                v[rows, :] = flat[at : at + 96, WIN:]

    for piece in range(2):
        along_y(1, piece).start()
        along_y(2, piece).start()
    for piece in range(2):
        over_z(0, piece).start()
        to_sibling(0, 0, piece).start()
    for load in loads[1:4]:
        load.wait()
    for load in loads[4:7]:
        load.start()
    project(0, 0, 1)
    arrive(1, 0)
    arrive(2, 0)
    for piece in range(2):
        along_y(3, piece).start()
    arrive(1, 1)
    arrive(2, 1)
    project(0, 1, 2, (0,))
    pass_z(0)
    project(0, 1, 2, (1,))
    arrive(3, 0)
    arrive(3, 1)
    project(1, 0, 1)
    pl.semaphore_wait(meet_sem.at[0], 3)
    pl.semaphore_signal(meet_sem.at[1], inc=1, device_id=opposite, device_id_type=MESH)

    def starts(j):
        return ((16 * j + 64 * core, 255), (16 * j + 72 + 64 * core, 0))

    def early(part, count):
        for j in range(4):
            window = slice(128 * j, 128 * j + 256)
            queries = q[part + (slice(None), slice(None), window)]
            shape = queries.shape[:3]
            queries, keys, values = queries.reshape(count, 256), k[:EARLY, window], v[:EARLY, window]
            for odd, (start, free) in enumerate(starts(j)):
                scores = nt_dot(choose(queries, head_lanes(start)), keys)
                top = jnp.max(scores, axis=-1, keepdims=True)
                weights = jnp.exp2(scores - top).astype(jnp.bfloat16)
                total = nn_dot(weights, count_in(values, free))
                first[(2 * j + odd,) + part] = total.reshape(shape + (256,))
                stat[(2 * j + odd,) + part] = jnp.broadcast_to(top, (count, 128)).reshape(shape + (128,))

    def late(g, j, carry):
        window = slice(128 * j, 128 * j + 256)
        queries = q[:, :, g, :, window].reshape(256, 256)
        keys, values = k[EARLY:, window], v[EARLY:, window]
        both = jnp.zeros((256, 256), jnp.float32)
        for odd, (start, free) in enumerate(starts(j)):
            h = 2 * j + odd
            mine = head_lanes(start)
            scores = nt_dot(choose(queries, mine), keys)
            parts = [scores[:, 128 * n : 128 * n + 128] for n in range(LATE // 128)]
            top = parts[0]
            for piece in parts[1:]:
                top = jnp.maximum(top, piece)
            before = stat[h, :, :, g].reshape(256, 128)
            top = jnp.maximum(before, jnp.max(top, axis=-1, keepdims=True))
            weights = jnp.concatenate([jnp.exp2(piece - top).astype(jnp.bfloat16) for piece in parts], axis=1)
            part = nn_dot(weights, count_in(values, free))
            shrink = jnp.exp2(before - top)
            earlier = first[h, :, :, g].reshape(256, 256)
            total = jnp.concatenate(
                [part[:, :128] + earlier[:, :128] * shrink, part[:, 128:] + earlier[:, 128:] * shrink], axis=1
            )
            both = jnp.where(mine, total * (1.0 / total[:, free : free + 1]), both)
        att[g, :, 128 * j : 128 * j + 128] = (carry + both[:, :128]).astype(jnp.bfloat16)
        if j == 3:
            att[g, :, 512:] = both[:, 128:].astype(jnp.bfloat16)
        return both[:, 128:]

    def swap(g):
        return remote(att.at[g, pl.ds(128, 128)], att_in.at[g], a_send.at[g], a_recv.at[g], sibling)

    def give(g, slot):
        return remote(u.at[g, slot], gathered.at[g, y], u_send.at[g, slot], u_recv.at[g, slot], along(STEPS[slot]))

    def own_give(g):
        return pltpu.make_async_copy(u.at[g, 0], gathered.at[g, y], own_sem.at[0, g])

    def finish(g):
        swap(g).wait_recv()
        mine = pl.ds(pl.multiple_of(core * 512, 128), WIN)
        other = pl.ds(pl.multiple_of((1 - core) * 512, 128), WIN)
        flat = nn_dot(att[g, :128], wo[mine, :]) + nn_dot(att_in[g], wo[other, :])
        values = x[:, pl.ds(pl.multiple_of(g * 32, 32), 32), :].astype(jnp.float32)
        u[g] = (values + table[2] * flat.reshape(4, 32, D)).astype(jnp.bfloat16)
        for slot in range(1, 4):
            give(g, slot).start()
        own_give(g).start()

    project(0, 3, 1)
    early((0, slice(0, 4)), 384)
    pass_z(1)
    pass_z(2)
    early((1, slice(0, 4)), 384)
    project(1, 1, 2)
    pass_z(3)
    project(1, 3, 1)
    loads[4].wait()

    def turn(g, carry):
        edge = jnp.zeros((256, 128), jnp.float32)
        edge = late(g, 0, edge)
        edge = late(g, 1, edge)

        @pl.when(g > 0)
        def _():
            finish(g - 1)

        edge = late(g, 2, edge)
        late(g, 3, edge)
        swap(g).start()
        return carry

    lax.fori_loop(0, 3, turn, 0)

    def spread(g, step):
        return remote(
            grouped.at[g, peer_frame(step)], t.at[g, frame], g_send.at[g, step], g_recv.at[g, step], peer(step)
        )

    def own_spread(g):
        return pltpu.make_async_copy(grouped.at[g, frame], t.at[g, frame], own_sem.at[1, g])

    def collect(g, step):
        return remote(r.at[g, peer_frame(step)], out.at[g, frame], r_send.at[g, step], r_recv.at[g, step], peer(step))

    def own_collect(g):
        return pltpu.make_async_copy(r.at[g, frame], out.at[g, frame], own_sem.at[2, g])

    forward = shuffle(True)
    pl.semaphore_wait(meet_sem.at[1], 1)

    def relay(g, carry):
        own_give(g).wait()
        for slot in range(1, 4):
            give(g, slot).wait_recv()
        grouped[g] = nn_dot(forward, gathered[g].reshape(128, D)).astype(jnp.bfloat16).reshape(8, 16, D)
        for step in FAR_FIRST:
            spread(g, step).start()
        own_spread(g).start()
        return carry

    relay(0, 0)
    finish(2)
    lax.fori_loop(1, 3, relay, 0)
    loads[5].wait()
    loads[6].wait()

    a = lax.broadcasted_iota(jnp.int32, (128, 128), 0)
    b = lax.broadcasted_iota(jnp.int32, (128, 128), 1)
    bias = jnp.where(a % 4 == b % 4, 0.0, -1e30)
    table1 = [mod[part, 1:2, :] for part in range(3)]

    def block(g, carry):
        own_spread(g).wait()
        for step in range(1, 8):
            spread(g, step).wait_recv()
        values = t[g].reshape(128, D)
        mixed = modulate(values, table1)
        packed[:, :D] = (nn_dot(mixed, wt[:, :D]) * SCALE).astype(jnp.bfloat16)
        packed[:, D : 2 * D] = nn_dot(mixed, wt[:, D : 2 * D]).astype(jnp.bfloat16)
        packed[:, 2 * D :] = nn_dot(mixed, wt[:, 2 * D :]).astype(jnp.bfloat16)
        spots = []
        scores = []
        for h in range(HEADS):
            at = 128 * min(HEAD * h // 128, 7)
            start = HEAD * h - at
            spots.append((at, head_lanes(start), 0 if start else 255))
            queries = choose(packed[:, at : at + 256], spots[h][1])
            scores.append(nt_dot(queries, packed[:, D + at : D + at + 256]) + bias)
        weights = []
        for h in range(HEADS):
            top = jnp.max(scores[h], axis=-1, keepdims=True)
            weights.append(jnp.exp2(scores[h] - top).astype(jnp.bfloat16))
        tiles = [None] * 9
        for h, (at, mine, free) in enumerate(spots):
            part = nn_dot(weights[h], count_in(packed[:, 2 * D + at : 2 * D + at + 256], free))
            part = jnp.where(mine, part * (1.0 / part[:, free : free + 1]), 0.0)
            for side in range(2):
                tile = at // 128 + side
                piece = part[:, 128 * side : 128 * side + 128]
                tiles[tile] = piece if tiles[tile] is None else tiles[tile] + piece
        for tile in range(9):
            mixed_t[:, 128 * tile : 128 * tile + 128] = tiles[tile].astype(jnp.bfloat16)
        flat = nn_dot(mixed_t[...], wto[...])
        r[g] = (values.astype(jnp.float32) + table1[2] * flat).astype(jnp.bfloat16).reshape(8, 16, D)
        for step in FAR_FIRST:
            collect(g, step).start()
        own_collect(g).start()
        return carry

    lax.fori_loop(0, 3, block, 0)

    def settle(g, carry):
        own_collect(g).wait()
        for step in range(1, 8):
            collect(g, step).wait_recv()
        return carry

    lax.fori_loop(0, 3, settle, 0)

    for piece in range(2):
        along_y(1, piece).wait_send()
        along_y(2, piece).wait_send()
        along_y(3, piece).wait_send()
        for slot in range(4):
            over_z(slot, piece).wait_send()
            to_sibling(0, slot, piece).wait_send()
            to_sibling(1, slot, piece).wait_send()

    def drain(g, carry):
        swap(g).wait_send()
        for slot in range(1, 4):
            give(g, slot).wait_send()
        for step in range(1, 8):
            spread(g, step).wait_send()
            collect(g, step).wait_send()
        return carry

    lax.fori_loop(0, 3, drain, 0)


def reorder(back, out):
    backward = shuffle(False)
    for g in range(3):
        rows = nn_dot(backward, back[g].reshape(128, D)).astype(jnp.bfloat16)
        out[:, g * 32 : g * 32 + 32, :] = rows.reshape(4, 32, D)


def shards(tokens, modulation, spatial_input, spatial_output, temporal_input, temporal_output):
    dma = pltpu.SemaphoreType.DMA
    held = pl.BlockSpec(memory_space=pl.ANY)

    def bf16(*shape):
        return pltpu.VMEM(shape, jnp.bfloat16)

    back = pl.pallas_call(
        kernel,
        out_shape=jax.ShapeDtypeStruct((3, 8, 16, D), jnp.bfloat16),
        in_specs=[held] * 6,
        out_specs=held,
        scratch_shapes=[
            pltpu.VMEM((3, 2, D), jnp.float32),
            bf16(4, 96, D),
            bf16(2, 4, 2, 96, D),
            bf16(D, 3 * WIN),
            bf16(D, D),
            bf16(2, 4, 3, 32, WIN),
            bf16(1536, WIN),
            bf16(1536, WIN),
            pltpu.VMEM((8, 2, 4, 3, 32, 256), jnp.float32),
            pltpu.VMEM((8, 2, 4, 3, 32, 128), jnp.float32),
            bf16(3, 256, WIN),
            bf16(3, 128, WIN),
            bf16(3, 4, 32, D),
            bf16(3, 4, 32, D),
            bf16(D, 3 * D),
            bf16(D, D),
            bf16(3, 8, 16, D),
            bf16(3, 8, 16, D),
            bf16(128, 3 * D),
            bf16(128, D),
            bf16(3, 8, 16, D),
            dma((8,)),
            dma((4, 2)), dma((4, 2)),
            dma((2, 4, 2)), dma((2, 4, 2)),
            dma((4, 2)), dma((4, 2)),
            dma((3,)), dma((3,)),
            dma((3, 4)), dma((3, 4)),
            dma((3, 8)), dma((3, 8)),
            dma((3, 8)), dma((3, 8)),
            dma((3, 3)),
            pltpu.SemaphoreType.REGULAR((2,)),
        ],
        compiler_params=pltpu.CompilerParams(
            collective_id=0, has_side_effects=True, vmem_limit_bytes=VMEM_LIMIT
        ),
        name="block_pair",
    )(tokens, jnp.transpose(modulation, (1, 0, 2)), spatial_input, spatial_output, temporal_input, temporal_output)
    vmem = pl.BlockSpec(memory_space=pltpu.VMEM)
    return pl.pallas_call(
        reorder,
        out_shape=jax.ShapeDtypeStruct((4, 96, D), jnp.bfloat16),
        in_specs=[vmem],
        out_specs=vmem,
        compiler_params=pltpu.CompilerParams(vmem_limit_bytes=VMEM_LIMIT),
        name="reorder",
    )(back)


def solution(mesh):
    in_specs = (P("frame", "patch", None), P(), P(), P(), P(), P())
    out_specs = P("frame", "patch", None)
    return jax.shard_map(shards, mesh=mesh, in_specs=in_specs, out_specs=out_specs, check_vma=False)
```

```python
import math

import jax
import jax.numpy as jnp
from jax import lax
from jax.experimental import pallas as pl
from jax.experimental.pallas import tpu as pltpu
from jax.sharding import PartitionSpec as P

D = 1152
HEADS = 16
HEAD = 72
WIN = 640
EARLY = 768
LATE = 768
PLACES = ((0, 1, 2, 4), (3, 5, 6, 7))
SCALE = math.log2(math.e) / math.sqrt(HEAD)
MESH = pl.DeviceIdType.MESH
VMEM_LIMIT = 60 * 1024 * 1024
FAR_FIRST = (6, 5, 2, 7, 1, 4, 3)
STEPS = (0, 1, 3, 2)


def modulate(values, table):
    wide = values.astype(jnp.float32)
    centre = jnp.mean(wide, axis=-1, keepdims=True)
    wide = wide - centre
    spread = jnp.mean(jnp.square(wide), axis=-1, keepdims=True)
    normed = wide * lax.rsqrt(spread + 1e-06)
    return (normed * (1.0 + table[1]) + table[0]).astype(jnp.bfloat16)


def nt_dot(a, b):
    return lax.dot_general(a, b, (((1,), (1,)), ((), ())), preferred_element_type=jnp.float32)


def nn_dot(a, b):
    return jnp.dot(a, b, preferred_element_type=jnp.float32)


def lanes(width):
    return lax.broadcasted_iota(jnp.int32, (1, width), 1)


def head_lanes(start):
    return (lanes(256) >= start) & (lanes(256) < start + HEAD)


def choose(queries, mine):
    return queries * jnp.where(mine, 1.0, 0.0).astype(jnp.bfloat16)


def count_in(values, free):
    one = jnp.where(lanes(256) == free, 1.0, 0.0)
    return values * (1.0 - one).astype(jnp.bfloat16) + one.astype(jnp.bfloat16)


def shuffle(forward):
    a = lax.broadcasted_iota(jnp.int32, (128, 128), 0)
    b = lax.broadcasted_iota(jnp.int32, (128, 128), 1)
    grouped, plain = (a, b) if forward else (b, a)
    source = ((grouped // 4) % 4) * 32 + (grouped // 16) * 4 + grouped % 4
    return jnp.where(source == plain, 1.0, 0.0).astype(jnp.bfloat16)


def kernel(
    tok, mod_in, w_in0, w_out0, w_in1, w_out1, out,
    mod, x, m, w, wo, q, k, v, first, stat, att, att_in, u, gathered,
    wt, wto, grouped, t, packed, mixed_t, r,
    load_sem, y_send, y_recv, s_send, s_recv, z_send, z_recv, a_send, a_recv,
    u_send, u_recv, g_send, g_recv, r_send, r_recv, own_sem, meet_sem,
):
    frame = lax.axis_index("frame")
    patch = lax.axis_index("patch")
    y = patch // 4
    z = (patch // 2) % 2
    core = patch % 2
    sibling = (frame, y * 4 + z * 2 + (1 - core))
    across = (frame, y * 4 + (1 - z) * 2 + core)

    def along(step):
        return (frame, ((y + step) % 4) * 4 + z * 2 + core)

    def peer_frame(step):
        return ((frame // 4 + step // 4) % 2) * 4 + (frame + step % 4) % 4

    def peer(step):
        return (peer_frame(step), patch)

    def beside_x(step):
        return ((frame // 4) * 4 + (frame + step) % 4, patch)

    opposite = ((frame + 4) % 8, patch)
    over_edge = ((frame + 4) % 8, y * 4 + (1 - z) * 2 + core)

    loads = [pltpu.make_async_copy(tok.at[y], x.at[0], load_sem.at[0])]
    for part in range(3):
        columns = pl.ds(pl.multiple_of(part * D + core * 512, 128), WIN)
        loads.append(
            pltpu.make_async_copy(w_in0.at[:, columns], w.at[:, pl.ds(part * WIN, WIN)], load_sem.at[1 + part])
        )
    loads.append(pltpu.make_async_copy(w_out0, wo, load_sem.at[4]))
    loads.append(pltpu.make_async_copy(w_in1, wt, load_sem.at[5]))
    loads.append(pltpu.make_async_copy(w_out1, wto, load_sem.at[6]))
    loads.append(pltpu.make_async_copy(mod_in, mod, load_sem.at[7]))
    for load in [loads[7]] + loads[:4]:
        load.start()

    barrier = pltpu.get_barrier_semaphore()
    beside = [beside_x(1), beside_x(3)]
    greeted = [sibling, across] + [along(s) for s in (1, 2, 3)] + beside + [over_edge]
    for device in greeted:
        pl.semaphore_signal(barrier, inc=1, device_id=device, device_id_type=MESH)
    loads[7].wait()
    table = [mod[part, 0:1, :] for part in range(3)]
    loads[0].wait()
    m[0, 0, 0] = modulate(x[0], table)
    pl.semaphore_wait(barrier, len(greeted))

    for device in beside + [across]:
        pl.semaphore_signal(meet_sem.at[0], inc=1, device_id=device, device_id_type=MESH)

    def remote(src, dst, send, recv, device):
        return pltpu.make_async_remote_copy(
            src_ref=src, dst_ref=dst, send_sem=send, recv_sem=recv, device_id=device, device_id_type=MESH
        )

    def rows_of(piece):
        return pl.ds(piece * 48, 48)

    def along_y(slot, piece):
        step = STEPS[slot]
        rows = rows_of(piece)
        return remote(
            tok.at[(y + 4 - step) % 4, rows], x.at[slot, rows],
            y_send.at[slot, piece], y_recv.at[slot, piece], along(4 - step),
        )

    def over_z(slot, piece):
        rows = rows_of(piece)
        return remote(
            m.at[0, slot, 0, rows], m.at[1, slot, 0, rows], z_send.at[slot, piece], z_recv.at[slot, piece], across
        )

    def to_sibling(half, slot, piece):
        rows = rows_of(piece)
        return remote(
            m.at[half, slot, 0, rows], m.at[half, slot, 1, rows],
            s_send.at[half, slot, piece], s_recv.at[half, slot, piece], sibling,
        )

    def arrive(slot, piece):
        along_y(slot, piece).wait_recv()
        rows = rows_of(piece)
        m[0, slot, 0, rows] = modulate(x[slot, rows], table)
        over_z(slot, piece).start()
        to_sibling(0, slot, piece).start()

    def pass_z(slot):
        for piece in range(2):
            over_z(slot, piece).wait_recv()
            to_sibling(1, slot, piece).start()

    def project(half, slot, count, quarters=(0, 1)):
        if 1 in quarters:
            for n in range(count):
                for piece in range(2):
                    to_sibling(half, slot + n, piece).wait_recv()
        chosen = slice(quarters[0], quarters[-1] + 1)
        mixed = m[half, slot : slot + count, chosen].reshape(96 * len(quarters) * count, D)
        flat = nn_dot(mixed, w[...] if half == 0 else w[:, WIN:])
        if half == 0:
            queries = (flat[:, :WIN] * SCALE).astype(jnp.bfloat16)
            flat = flat[:, WIN:]
        flat = flat.astype(jnp.bfloat16)
        for n in range(count):
            for index, quarter in enumerate(quarters):
                at = (n * len(quarters) + index) * 96
                if half == 0:
                    q[quarter, slot + n] = queries[at : at + 96].reshape(3, 32, WIN)
                rows = pl.ds(PLACES[half][slot + n] * 192 + quarter * 96, 96)
                k[rows, :] = flat[at : at + 96, :WIN]
                v[rows, :] = flat[at : at + 96, WIN:]

    for piece in range(2):
        along_y(1, piece).start()
        along_y(2, piece).start()
    for piece in range(2):
        over_z(0, piece).start()
        to_sibling(0, 0, piece).start()
    for load in loads[1:4]:
        load.wait()
    for load in loads[4:7]:
        load.start()
    project(0, 0, 1)
    arrive(1, 0)
    arrive(2, 0)
    for piece in range(2):
        along_y(3, piece).start()
    arrive(1, 1)
    arrive(2, 1)
    project(0, 1, 2, (0,))
    pass_z(0)
    project(0, 1, 2, (1,))
    project(1, 0, 1)
    pl.semaphore_wait(meet_sem.at[0], 3)
    pl.semaphore_signal(meet_sem.at[1], inc=1, device_id=opposite, device_id_type=MESH)

    def starts(j):
        return ((16 * j + 64 * core, 255), (16 * j + 72 + 64 * core, 0))

    def early(part, count):
        for j in range(4):
            window = slice(128 * j, 128 * j + 256)
            queries = q[part + (slice(None), slice(None), window)]
            shape = queries.shape[:3]
            queries, keys, values = queries.reshape(count, 256), k[:EARLY, window], v[:EARLY, window]
            for odd, (start, free) in enumerate(starts(j)):
                scores = nt_dot(choose(queries, head_lanes(start)), keys)
                top = jnp.max(scores, axis=-1, keepdims=True)
                weights = jnp.exp2(scores - top).astype(jnp.bfloat16)
                total = nn_dot(weights, count_in(values, free))
                first[(2 * j + odd,) + part] = total.reshape(shape + (256,))
                stat[(2 * j + odd,) + part] = jnp.broadcast_to(top, (count, 128)).reshape(shape + (128,))

    def late(g, j, carry):
        window = slice(128 * j, 128 * j + 256)
        queries = q[:, :, g, :, window].reshape(256, 256)
        keys, values = k[EARLY:, window], v[EARLY:, window]
        both = jnp.zeros((256, 256), jnp.float32)
        for odd, (start, free) in enumerate(starts(j)):
            h = 2 * j + odd
            mine = head_lanes(start)
            scores = nt_dot(choose(queries, mine), keys)
            parts = [scores[:, 128 * n : 128 * n + 128] for n in range(LATE // 128)]
            top = parts[0]
            for piece in parts[1:]:
                top = jnp.maximum(top, piece)
            before = stat[h, :, :, g].reshape(256, 128)
            top = jnp.maximum(before, jnp.max(top, axis=-1, keepdims=True))
            weights = jnp.concatenate([jnp.exp2(piece - top).astype(jnp.bfloat16) for piece in parts], axis=1)
            part = nn_dot(weights, count_in(values, free))
            shrink = jnp.exp2(before - top)
            earlier = first[h, :, :, g].reshape(256, 256)
            total = jnp.concatenate(
                [part[:, :128] + earlier[:, :128] * shrink, part[:, 128:] + earlier[:, 128:] * shrink], axis=1
            )
            both = jnp.where(mine, total * (1.0 / total[:, free : free + 1]), both)
        att[g, :, 128 * j : 128 * j + 128] = (carry + both[:, :128]).astype(jnp.bfloat16)
        if j == 3:
            att[g, :, 512:] = both[:, 128:].astype(jnp.bfloat16)
        return both[:, 128:]

    def swap(g):
        return remote(att.at[g, pl.ds(128, 128)], att_in.at[g], a_send.at[g], a_recv.at[g], sibling)

    def give(g, slot):
        return remote(u.at[g, slot], gathered.at[g, y], u_send.at[g, slot], u_recv.at[g, slot], along(STEPS[slot]))

    def own_give(g):
        return pltpu.make_async_copy(u.at[g, 0], gathered.at[g, y], own_sem.at[0, g])

    def finish(g):
        swap(g).wait_recv()
        mine = pl.ds(pl.multiple_of(core * 512, 128), WIN)
        other = pl.ds(pl.multiple_of((1 - core) * 512, 128), WIN)
        flat = nn_dot(att[g, :128], wo[mine, :]) + nn_dot(att_in[g], wo[other, :])
        values = x[:, pl.ds(pl.multiple_of(g * 32, 32), 32), :].astype(jnp.float32)
        u[g] = (values + table[2] * flat.reshape(4, 32, D)).astype(jnp.bfloat16)
        for slot in range(1, 4):
            give(g, slot).start()
        own_give(g).start()

    arrive(3, 0)
    arrive(3, 1)
    early((0, slice(0, 3)), 288)
    early((1, slice(0, 3)), 288)
    project(0, 3, 1)
    pass_z(1)
    pass_z(2)
    early((slice(0, 2), 3), 192)
    project(1, 1, 2)
    pass_z(3)
    project(1, 3, 1)
    loads[4].wait()

    def turn(g, carry):
        edge = jnp.zeros((256, 128), jnp.float32)
        edge = late(g, 0, edge)
        edge = late(g, 1, edge)

        @pl.when(g > 0)
        def _():
            finish(g - 1)

        edge = late(g, 2, edge)
        late(g, 3, edge)
        swap(g).start()
        return carry

    lax.fori_loop(0, 3, turn, 0)

    def spread(g, step):
        return remote(
            grouped.at[g, peer_frame(step)], t.at[g, frame], g_send.at[g, step], g_recv.at[g, step], peer(step)
        )

    def own_spread(g):
        return pltpu.make_async_copy(grouped.at[g, frame], t.at[g, frame], own_sem.at[1, g])

    def collect(g, step):
        return remote(r.at[g, peer_frame(step)], out.at[g, frame], r_send.at[g, step], r_recv.at[g, step], peer(step))

    def own_collect(g):
        return pltpu.make_async_copy(r.at[g, frame], out.at[g, frame], own_sem.at[2, g])

    forward = shuffle(True)
    pl.semaphore_wait(meet_sem.at[1], 1)

    def relay(g, carry):
        own_give(g).wait()
        for slot in range(1, 4):
            give(g, slot).wait_recv()
        grouped[g] = nn_dot(forward, gathered[g].reshape(128, D)).astype(jnp.bfloat16).reshape(8, 16, D)
        for step in FAR_FIRST:
            spread(g, step).start()
        own_spread(g).start()
        return carry

    relay(0, 0)
    finish(2)
    lax.fori_loop(1, 3, relay, 0)
    loads[5].wait()
    loads[6].wait()

    a = lax.broadcasted_iota(jnp.int32, (128, 128), 0)
    b = lax.broadcasted_iota(jnp.int32, (128, 128), 1)
    bias = jnp.where(a % 4 == b % 4, 0.0, -1e30)
    table1 = [mod[part, 1:2, :] for part in range(3)]

    def block(g, carry):
        own_spread(g).wait()
        for step in range(1, 8):
            spread(g, step).wait_recv()
        values = t[g].reshape(128, D)
        mixed = modulate(values, table1)
        packed[:, :D] = (nn_dot(mixed, wt[:, :D]) * SCALE).astype(jnp.bfloat16)
        packed[:, D : 2 * D] = nn_dot(mixed, wt[:, D : 2 * D]).astype(jnp.bfloat16)
        packed[:, 2 * D :] = nn_dot(mixed, wt[:, 2 * D :]).astype(jnp.bfloat16)
        spots = []
        scores = []
        for h in range(HEADS):
            at = 128 * min(HEAD * h // 128, 7)
            start = HEAD * h - at
            spots.append((at, head_lanes(start), 0 if start else 255))
            queries = choose(packed[:, at : at + 256], spots[h][1])
            scores.append(nt_dot(queries, packed[:, D + at : D + at + 256]) + bias)
        weights = []
        for h in range(HEADS):
            top = jnp.max(scores[h], axis=-1, keepdims=True)
            weights.append(jnp.exp2(scores[h] - top).astype(jnp.bfloat16))
        tiles = [None] * 9
        for h, (at, mine, free) in enumerate(spots):
            part = nn_dot(weights[h], count_in(packed[:, 2 * D + at : 2 * D + at + 256], free))
            part = jnp.where(mine, part * (1.0 / part[:, free : free + 1]), 0.0)
            for side in range(2):
                tile = at // 128 + side
                piece = part[:, 128 * side : 128 * side + 128]
                tiles[tile] = piece if tiles[tile] is None else tiles[tile] + piece
        for tile in range(9):
            mixed_t[:, 128 * tile : 128 * tile + 128] = tiles[tile].astype(jnp.bfloat16)
        flat = nn_dot(mixed_t[...], wto[...])
        r[g] = (values.astype(jnp.float32) + table1[2] * flat).astype(jnp.bfloat16).reshape(8, 16, D)
        for step in FAR_FIRST:
            collect(g, step).start()
        own_collect(g).start()
        return carry

    lax.fori_loop(0, 3, block, 0)

    def settle(g, carry):
        own_collect(g).wait()
        for step in range(1, 8):
            collect(g, step).wait_recv()
        return carry

    lax.fori_loop(0, 3, settle, 0)

    for piece in range(2):
        along_y(1, piece).wait_send()
        along_y(2, piece).wait_send()
        along_y(3, piece).wait_send()
        for slot in range(4):
            over_z(slot, piece).wait_send()
            to_sibling(0, slot, piece).wait_send()
            to_sibling(1, slot, piece).wait_send()

    def drain(g, carry):
        swap(g).wait_send()
        for slot in range(1, 4):
            give(g, slot).wait_send()
        for step in range(1, 8):
            spread(g, step).wait_send()
            collect(g, step).wait_send()
        return carry

    lax.fori_loop(0, 3, drain, 0)


def reorder(back, out):
    backward = shuffle(False)
    for g in range(3):
        rows = nn_dot(backward, back[g].reshape(128, D)).astype(jnp.bfloat16)
        out[:, g * 32 : g * 32 + 32, :] = rows.reshape(4, 32, D)


def shards(tokens, modulation, spatial_input, spatial_output, temporal_input, temporal_output):
    dma = pltpu.SemaphoreType.DMA
    held = pl.BlockSpec(memory_space=pl.ANY)

    def bf16(*shape):
        return pltpu.VMEM(shape, jnp.bfloat16)

    back = pl.pallas_call(
        kernel,
        out_shape=jax.ShapeDtypeStruct((3, 8, 16, D), jnp.bfloat16),
        in_specs=[held] * 6,
        out_specs=held,
        scratch_shapes=[
            pltpu.VMEM((3, 2, D), jnp.float32),
            bf16(4, 96, D),
            bf16(2, 4, 2, 96, D),
            bf16(D, 3 * WIN),
            bf16(D, D),
            bf16(2, 4, 3, 32, WIN),
            bf16(1536, WIN),
            bf16(1536, WIN),
            pltpu.VMEM((8, 2, 4, 3, 32, 256), jnp.float32),
            pltpu.VMEM((8, 2, 4, 3, 32, 128), jnp.float32),
            bf16(3, 256, WIN),
            bf16(3, 128, WIN),
            bf16(3, 4, 32, D),
            bf16(3, 4, 32, D),
            bf16(D, 3 * D),
            bf16(D, D),
            bf16(3, 8, 16, D),
            bf16(3, 8, 16, D),
            bf16(128, 3 * D),
            bf16(128, D),
            bf16(3, 8, 16, D),
            dma((8,)),
            dma((4, 2)), dma((4, 2)),
            dma((2, 4, 2)), dma((2, 4, 2)),
            dma((4, 2)), dma((4, 2)),
            dma((3,)), dma((3,)),
            dma((3, 4)), dma((3, 4)),
            dma((3, 8)), dma((3, 8)),
            dma((3, 8)), dma((3, 8)),
            dma((3, 3)),
            pltpu.SemaphoreType.REGULAR((2,)),
        ],
        compiler_params=pltpu.CompilerParams(
            collective_id=0, has_side_effects=True, vmem_limit_bytes=VMEM_LIMIT
        ),
        name="block_pair",
    )(tokens, jnp.transpose(modulation, (1, 0, 2)), spatial_input, spatial_output, temporal_input, temporal_output)
    vmem = pl.BlockSpec(memory_space=pltpu.VMEM)
    return pl.pallas_call(
        reorder,
        out_shape=jax.ShapeDtypeStruct((4, 96, D), jnp.bfloat16),
        in_specs=[vmem],
        out_specs=vmem,
        compiler_params=pltpu.CompilerParams(vmem_limit_bytes=VMEM_LIMIT),
        name="reorder",
    )(back)


def solution(mesh):
    in_specs = (P("frame", "patch", None), P(), P(), P(), P(), P())
    out_specs = P("frame", "patch", None)
    return jax.shard_map(shards, mesh=mesh, in_specs=in_specs, out_specs=out_specs, check_vma=False)
```
